256 devices in a mesh: seq: 8 (over y, core), tp: 8 (over z), dp: 4 (over x).
Axes of the slice: x: 4, y: 4, z: 8, core: 2. Of those that a mesh axis runs over, the one named last changes fastest.
Arguments:
- queries: bfloat16 [16384, 4096], P(('seq', 'dp'), 'tp'), may hold values from -6 to 6
- keys: bfloat16 [16384, 4096], P(('seq', 'dp'), 'tp'), may hold values from -6 to 6
- values: bfloat16 [16384, 4096], P(('seq', 'dp'), 'tp'), may hold values from -6 to 6
- gain: float32 [4096], P('tp'), may hold values from 0.5 to 2
- out_weight: bfloat16 [4096, 4096], P(('seq', 'dp'), 'tp'), may hold values from -0.09375 to 0.09375
- out_cotangent: bfloat16 [16384, 4096], P(('seq', 'dp'), 'tp'), may hold values from -6 to 6
Outputs:
- query_grad: bfloat16 [16384, 4096], P(('seq', 'dp'), 'tp')
- key_grad: bfloat16 [16384, 4096], P(('seq', 'dp'), 'tp')
- value_grad: bfloat16 [16384, 4096], P(('seq', 'dp'), 'tp')
- gain_grad: float32 [4096], P('tp')
- weight_grad: float32 [4096, 4096], P(('seq', 'dp'), 'tp')
The draws below stay inside these ranges and needn't reach their ends.
All inputs are finite; a program needn't handle non-finite values.
Results may differ from the reference program's by a relative error of at most 0.023.
Values may be sent and summed in bfloat16 or wider, within the bound.
No kernel may reach another device: no remote copies, remote signals or barrier semaphores. Data moves between devices by JAX's collectives and lax.ppermute only.
A program may use at most 128 MiB of HBM per device.

```python
import math
import jax
import jax.numpy as jnp
from jax import lax

D = 4096
HEADS = 32
HEAD_DIM = 128
TOK_DEV = 512
HD = 4096
TOKENS = 16384


def spiked(result, stream_key, source, target, shards_of, factor):
    owner, partner = [(jnp.arange(result.shape[axis_at]) // (result.shape[axis_at] // shards_of)).reshape([-1 if axis == axis_at else 1 for axis in range(result.ndim)]) for axis_at in (source, target)]
    chosen = jax.random.permutation(stream_key, shards_of)[partner]
    strong = (owner == chosen) | (owner == (partner + shards_of // 2) % shards_of)
    return jnp.where(strong, factor * result, result)


def levels(own_key, extent, cuts, smallest, high):
    loudness = 1.0
    for dim, shards_of in cuts:
        heights = jax.random.uniform(jax.random.fold_in(jax.random.fold_in(own_key, 6), dim), (shards_of,), jnp.float32, smallest / len(cuts), high / len(cuts))
        loudness = loudness * jnp.repeat(jnp.exp(heights), extent[dim] // shards_of).reshape((-1,) + (1,) * (len(extent) - 1 - dim))
    return loudness


def noise(own_key, shape, spread, bound, pieces=(), held_as=jnp.bfloat16):
    result = jax.random.normal(own_key, shape, jnp.float32) * spread
    if len(pieces) > 0:
        result = levels(own_key, shape, pieces, -0.22, 0.18) * result
    return jnp.clip(result, min=-bound, max=bound).astype(held_as)


def bell_draw_with(own_key, dims, spread, most, pieces, heavy, held_as=jnp.bfloat16):
    result = spread * jax.random.normal(own_key, dims, jnp.float32)
    if pieces:
        result = result * levels(own_key, dims, pieces, -0.22, 0.18)
    return jnp.clip(spiked(result, jax.random.fold_in(own_key, 3), *heavy), -most, most).astype(held_as)


def setup_inputs(seed: int = 0) -> dict:
    splits = jax.random.split(jax.random.key(seed), 7)
    return {
        "queries": noise(splits[0], (TOKENS, HD), 1.0, 6.0, ((0, 32), (1, 8))),
        "keys": noise(splits[1], (TOKENS, HD), 1.0, 6.0, ((0, 32), (1, 8))),
        "values": noise(splits[2], (TOKENS, HD), 1.0, 6.0, ((0, 32), (1, 8))),
        "gain": jnp.clip(jnp.exp(math.log(2.0) - 1.3862944 * jax.random.uniform(splits[3], (HD,), jnp.float32) ** levels(splits[3], (HD,), ((0, 8),), -0.2, 0.2)), 0.5, 2.0),
        "out_weight": noise(splits[4], (D, HD), D ** -0.5, 0.09375, ((0, 32), (1, 8))),
        "out_cotangent": bell_draw_with(splits[5], (TOKENS, D), 1.0, 6.0, ((0, 32), (1, 8)), (0, 1, 32, 2.75)),
    }


EPS = 1e-06

def round_bfloat(tensor):
    return lax.optimization_barrier(tensor.astype(jnp.bfloat16)).astype(jnp.float32)

def reference(queries, keys, values, gain, out_weight, out_cotangent):
    blocks = TOKENS // TOK_DEV
    shape_view = (blocks, TOK_DEV, HEADS, HEAD_DIM)
    query_h = queries.astype(jnp.float32).reshape(shape_view)
    key_h = keys.astype(jnp.float32).reshape(shape_view)
    value_h = values.astype(jnp.float32).reshape(shape_view)
    positions = jnp.arange(TOK_DEV)
    causal = positions[:, None] >= positions[None, :]
    state = jnp.einsum('cthi,cthj->chij', key_h, value_h)
    empty_state = jnp.zeros((1, HEADS, HEAD_DIM, HEAD_DIM), jnp.float32)
    running = jnp.cumsum(state, axis=0)
    prior_state = round_bfloat(jnp.concatenate([empty_state, running[:-1]], axis=0))
    scores = jnp.einsum('cthi,cshi->chts', query_h, key_h)
    scores = round_bfloat(jnp.where(causal, scores, 0.0))
    attended = jnp.einsum('chts,cshj->cthj', scores, value_h) + jnp.einsum('cthi,chij->cthj', query_h, prior_state)
    inverse_rms = lax.rsqrt(lax.optimization_barrier(jnp.mean(attended * attended, axis=-1, keepdims=True)) + EPS)
    normed = attended * inverse_rms
    gain_view = gain.reshape(HEADS, HEAD_DIM)
    gated = (normed * gain_view).reshape(TOKENS, HD).astype(jnp.bfloat16)
    grad_gated = jnp.dot(out_cotangent, out_weight, preferred_element_type=jnp.float32)
    gain_part = lax.optimization_barrier(jnp.sum(grad_gated * normed.reshape(TOKENS, HD), axis=0))
    weight_part = lax.dot_general(out_cotangent, gated, (((0,), (0,)), ((), ())), preferred_element_type=jnp.float32)
    grad_normed = grad_gated.reshape(shape_view) * gain_view
    grad_attended = (grad_normed - normed * lax.optimization_barrier(jnp.mean(grad_normed * normed, axis=-1, keepdims=True))) * inverse_rms
    grad_attended = round_bfloat(grad_attended)
    back_scores = jnp.einsum('cthj,cshj->chts', grad_attended, value_h)
    back_scores = round_bfloat(jnp.where(causal, back_scores, 0.0))
    grad_state = jnp.einsum('cthi,cthj->chij', query_h, grad_attended)
    reverse_run = jnp.cumsum(grad_state[::-1], axis=0)[::-1]
    later_state = round_bfloat(jnp.concatenate([reverse_run[1:], empty_state], axis=0))
    query_grad = jnp.einsum('chts,cshi->cthi', back_scores, key_h) + jnp.einsum('cthj,chij->cthi', grad_attended, prior_state)
    key_grad = jnp.einsum('chts,cthi->cshi', back_scores, query_h) + jnp.einsum('cshj,chij->cshi', value_h, later_state)
    value_grad = jnp.einsum('chts,cthj->cshj', scores, grad_attended) + jnp.einsum('cshi,chij->cshj', key_h, later_state)
    grad_scale = 1.0 / TOKENS ** 0.5
    return (query_grad.reshape(TOKENS, HD).astype(jnp.bfloat16), key_grad.reshape(TOKENS, HD).astype(jnp.bfloat16), value_grad.reshape(TOKENS, HD).astype(jnp.bfloat16), gain_part * grad_scale, weight_part * grad_scale)
```

```python
import math

import jax
import jax.numpy as jnp
from jax import lax
from jax.experimental import pallas as pl
from jax.experimental.pallas import tpu as pltpu
from jax.sharding import Mesh
from jax.sharding import PartitionSpec as P

HEAD_DIM = 128
HEADS = 4
TOKENS = 512
WIDTH = 512
EPS = 1e-06
BF = jnp.bfloat16
F32 = jnp.float32
PLANE = ("y", "dp")
BLOCKS = ("y", "core", "dp")
VMEM_LIMIT = 48 * 1024 * 1024


def dot(a, b, dims):
    return lax.dot_general(a, b, (dims, ((), ())), preferred_element_type=F32)


NN = ((1,), (0,))
NT = ((1,), (1,))
TN = ((0,), (0,))


def head(ref, h):
    return ref[:, h * HEAD_DIM : (h + 1) * HEAD_DIM]


def causal_mask():
    rows = lax.broadcasted_iota(jnp.int32, (TOKENS, TOKENS), 0)
    cols = lax.broadcasted_iota(jnp.int32, (TOKENS, TOKENS), 1)
    return rows >= cols


def call(kernel, out, n_in, flops, any_in=0, scratch=()):
    vmem = pl.BlockSpec(memory_space=pltpu.VMEM)
    anys = pl.BlockSpec(memory_space=pl.ANY)
    return pl.pallas_call(
        kernel,
        out_shape=tuple(jax.ShapeDtypeStruct(s, d) for s, d in out),
        in_specs=[anys] * any_in + [vmem] * n_in,
        out_specs=tuple(vmem for _ in out),
        scratch_shapes=scratch,
        compiler_params=pltpu.CompilerParams(vmem_limit_bytes=VMEM_LIMIT),
        cost_estimate=pl.CostEstimate(flops=flops, bytes_accessed=4 << 20, transcendentals=0),
    )


def state_kernel(k_ref, v_ref, out_ref):
    for h in range(HEADS):
        state = dot(head(k_ref, h), head(v_ref, h), TN).astype(BF)
        out_ref[h * 8 : (h + 1) * 8] = state.reshape(8, 16, HEAD_DIM)


def intra_kernel(q_ref, k_ref, v_ref, att_ref):
    mask = causal_mask()
    for h in range(HEADS):
        scores = dot(head(q_ref, h), head(k_ref, h), NT)
        scores = jnp.where(mask, scores, 0.0).astype(BF)
        att_ref[:, h * HEAD_DIM : (h + 1) * HEAD_DIM] = dot(scores, head(v_ref, h), NN)


def scan_kernel(in_ref, out_ref):
    total = jnp.zeros((16, HEAD_DIM), F32)
    for c in range(32):
        out_ref[c] = total.astype(BF)
        total = total + in_ref[c].astype(F32)


def scan_back_kernel(in_ref, out_ref, gain_ref):
    total = jnp.zeros((16, HEAD_DIM), F32)
    gain = jnp.zeros((16, HEAD_DIM), F32)
    for c in range(31, -1, -1):
        out_ref[c] = total.astype(BF)
        total = total + in_ref[c, 0:16].astype(F32)
        gain = gain + in_ref[c, 16:32].astype(F32)
    gain_ref[...] = (gain[0:4] + gain[4:8]) * (1.0 / math.sqrt(16384.0))


def norm_kernel(q_ref, prior_ref, gain_ref, intra_ref, att_ref, gated_ref):
    for h in range(HEADS):
        cols = slice(h * HEAD_DIM, (h + 1) * HEAD_DIM)
        prior = prior_ref[h * 8 : (h + 1) * 8].reshape(HEAD_DIM, HEAD_DIM)
        att = intra_ref[:, cols] + dot(q_ref[:, cols], prior, NN)
        att_ref[:, cols] = att
        inverse = lax.rsqrt(jnp.mean(att * att, axis=-1, keepdims=True) + EPS)
        gated = (att * inverse * gain_ref[:, cols]).astype(BF)
        gated_ref[cols, :] = gated.T


def load_rows(chunks, a_vmem, sems):
    place = lax.axis_index("tp")
    copies = []
    for i, k in enumerate((0, 1, -1, 2, -2, 3, -3)):
        j = lax.rem(place + 8 - k, 8)
        copies.append(pltpu.make_async_copy(chunks[i], a_vmem.at[j], sems.at[i]))
    j = lax.rem(place + 4, 8)
    half = TOKENS // 2
    copies.append(pltpu.make_async_copy(chunks[7], a_vmem.at[j, 0:half], sems.at[7]))
    copies.append(pltpu.make_async_copy(chunks[8], a_vmem.at[j, half:TOKENS], sems.at[8]))
    return copies


def weight_kernel(*refs):
    chunks, (gated_ref, mine_ref, other_ref, a_vmem, sems) = refs[:9], refs[9:]
    copies = load_rows(chunks, a_vmem, sems)
    for c in copies:
        c.start()
    for c in copies:
        c.wait()
    core = lax.axis_index("core")
    for out, parity in ((mine_ref, core), (other_ref, 1 - core)):
        for y in range(4):
            part = dot(gated_ref[...], a_vmem[2 * y + parity], NN).astype(BF)
            for x in range(4):
                out[4 * y + x] = part[:, x * 128 : (x + 1) * 128]


def grad_kernel(*refs):
    chunks, rest = refs[:9], refs[9:]
    wm, wo, q_ref, att_ref, gain_ref, ga_ref, send_ref, a_vmem, w_vmem, acc, sems, wsems = rest
    core = lax.axis_index("core")
    copies = load_rows(chunks, a_vmem, sems)
    for y in range(4):
        rows = slice(4 * y, 4 * y + 4)
        copies.append(pltpu.make_async_copy(wm.at[rows], w_vmem.at[2 * y + core], wsems.at[y]))
        copies.append(
            pltpu.make_async_copy(wo.at[rows], w_vmem.at[2 * y + 1 - core], wsems.at[4 + y])
        )
    for c in copies:
        c.start()
    for c in copies:
        c.wait()
    for j in range(8):
        part = dot(a_vmem[j], w_vmem[j].reshape(WIDTH, WIDTH), NN)
        acc[...] = part if j == 0 else acc[...] + part
    for h in range(HEADS):
        cols = slice(h * HEAD_DIM, (h + 1) * HEAD_DIM)
        att = att_ref[:, cols]
        inverse = lax.rsqrt(jnp.mean(att * att, axis=-1, keepdims=True) + EPS)
        normed = att * inverse
        grad = acc[:, cols]
        gain_part = jnp.sum(grad * normed, axis=0, keepdims=True)
        grad = grad * gain_ref[:, cols]
        grad = (grad - normed * jnp.mean(grad * normed, axis=-1, keepdims=True)) * inverse
        grad = grad.astype(BF)
        ga_ref[:, cols] = grad
        state = dot(q_ref[:, cols], grad, TN).astype(BF)
        send_ref[h * 8 : (h + 1) * 8, 0:16, :] = state.reshape(8, 16, HEAD_DIM)
        high = gain_part.astype(BF).astype(F32)
        low = gain_part - high
        acc[h : h + 1, 0:HEAD_DIM] = high
        acc[4 + h : 5 + h, 0:HEAD_DIM] = low
    acc[8:16, 0:HEAD_DIM] = jnp.zeros((8, HEAD_DIM), F32)
    rows = acc[0:16, 0:HEAD_DIM].astype(BF)
    for c in range(32):
        send_ref[c, 16:32, :] = rows


def post_kernel(q_ref, k_ref, v_ref, ga_ref, prior_ref, qg_ref, kp_ref, vp_ref):
    mask = causal_mask()
    for h in range(HEADS):
        cols = slice(h * HEAD_DIM, (h + 1) * HEAD_DIM)
        q, k, v, ga = q_ref[:, cols], k_ref[:, cols], v_ref[:, cols], ga_ref[:, cols]
        prior = prior_ref[h * 8 : (h + 1) * 8].reshape(HEAD_DIM, HEAD_DIM)
        scores = jnp.where(mask, dot(q, k, NT), 0.0).astype(BF)
        vp_ref[:, cols] = dot(scores, ga, TN)
        back = jnp.where(mask, dot(ga, v, NT), 0.0).astype(BF)
        qg_ref[:, cols] = (dot(back, k, NN) + dot(ga, prior, NT)).astype(BF)
        kp_ref[:, cols] = dot(back, q, TN)


def final_kernel(k_ref, v_ref, later_ref, kp_ref, vp_ref, kg_ref, vg_ref):
    for h in range(HEADS):
        cols = slice(h * HEAD_DIM, (h + 1) * HEAD_DIM)
        later = later_ref[h * 8 : (h + 1) * 8].reshape(HEAD_DIM, HEAD_DIM)
        kg_ref[:, cols] = (kp_ref[:, cols] + dot(v_ref[:, cols], later, NT)).astype(BF)
        vg_ref[:, cols] = (vp_ref[:, cols] + dot(k_ref[:, cols], later, NN)).astype(BF)


def sum_kernel(in_ref, out_ref):
    total = in_ref[0].astype(F32)
    for c in range(1, 16):
        total = total + in_ref[c].astype(F32)
    out_ref[...] = (total * (1.0 / math.sqrt(16384.0))).T


def around(n, k):
    return [(i, (i + k) % n) for i in range(n)]


def swap_cores(x):
    return lax.ppermute(x, "core", [(0, 1), (1, 0)])


def exchange(x, axes):
    return lax.all_to_all(x, axes, 0, 0, tiled=True)


def body(queries, keys, values, gain, out_weight, out_cotangent):
    square = (TOKENS, WIDTH)
    up, down = around(8, 1), around(8, -1)
    half = TOKENS // 2
    chunks = [out_cotangent]
    fwd = bwd = out_cotangent
    for _ in range(3):
        fwd = lax.ppermute(fwd, "tp", up)
        bwd = lax.ppermute(bwd, "tp", down)
        chunks += [fwd, bwd]
    chunks += [lax.ppermute(fwd[:half], "tp", up), lax.ppermute(bwd[half:], "tp", down)]

    (state,) = call(state_kernel, [((32, 16, 128), BF)], 2, 1 << 27)(keys, values)
    states = exchange(state, BLOCKS)
    (priors,) = call(scan_kernel, [((32, 16, 128), BF)], 1, 1 << 22)(states)
    prior = exchange(priors, BLOCKS)
    (intra,) = call(intra_kernel, [(square, F32)], 3, 1 << 30)(queries, keys, values)
    w_mine = exchange(jnp.broadcast_to(out_weight[None], (16, 128, WIDTH)), PLANE)
    w_other = swap_cores(w_mine)
    gain_row = gain.reshape(1, WIDTH)
    att, gated = call(norm_kernel, [(square, F32), (square, BF)], 4, 1 << 28)(
        queries, prior, gain_row, intra
    )
    rows_scratch = [pltpu.VMEM((8, TOKENS, WIDTH), BF)]
    mine, other = call(
        weight_kernel,
        [((16, WIDTH, 128), BF), ((16, WIDTH, 128), BF)],
        1,
        1 << 32,
        9,
        rows_scratch + [pltpu.SemaphoreType.DMA((9,))],
    )(*chunks, gated)
    ga, send = call(
        grad_kernel,
        [(square, BF), ((32, 32, 128), BF)],
        3,
        1 << 32,
        11,
        rows_scratch
        + [
            pltpu.VMEM((8, 4, 128, WIDTH), BF),
            pltpu.VMEM(square, F32),
            pltpu.SemaphoreType.DMA((9,)),
            pltpu.SemaphoreType.DMA((8,)),
        ],
    )(*chunks, w_mine, w_other, queries, att, gain_row)
    received = exchange(send, BLOCKS)
    laters, gain_sum = call(scan_back_kernel, [((32, 16, 128), BF), ((4, 128), F32)], 1, 1 << 22)(
        received
    )
    later = exchange(laters, BLOCKS)
    query_grad, key_part, value_part = call(
        post_kernel, [(square, BF), (square, F32), (square, F32)], 5, 1 << 31
    )(queries, keys, values, ga, prior)
    both = (mine.astype(F32) + swap_cores(other).astype(F32)).astype(BF)
    parts = exchange(both, PLANE)
    (weight_grad,) = call(sum_kernel, [((128, WIDTH), F32)], 1, 1 << 22)(parts)
    key_grad, value_grad = call(final_kernel, [(square, BF), (square, BF)], 5, 1 << 28)(
        keys, values, later, key_part, value_part
    )
    return query_grad, key_grad, value_grad, gain_sum.reshape(WIDTH), weight_grad


def solution(mesh):
    grid = Mesh(mesh.devices.reshape(4, 2, 8, 4), ("y", "core", "tp", "dp"))
    rows = P(("y", "core", "dp"), "tp")
    return jax.shard_map(
        body,
        mesh=grid,
        in_specs=(rows, rows, rows, P("tp"), rows, rows),
        out_specs=(rows, rows, rows, P("tp"), rows),
        check_vma=False,
    )
```

```python
import math

import jax
import jax.numpy as jnp
from jax import lax
from jax.experimental import pallas as pl
from jax.experimental.pallas import tpu as pltpu
from jax.sharding import Mesh
from jax.sharding import PartitionSpec as P

HEAD_DIM = 128
HEADS = 4
TOKENS = 512
WIDTH = 512
RING = 8
EPS = 1e-06
SCALE = 1.0 / math.sqrt(16384.0)
BF = jnp.bfloat16
F32 = jnp.float32
PLANE = ("y", "dp")
VMEM_LIMIT = 24 * 1024 * 1024
STATE = (HEADS * HEAD_DIM, HEAD_DIM)
STATE_GAIN = (HEADS * HEAD_DIM + 16, HEAD_DIM)
SQUARE = (TOKENS, WIDTH)

NN = ((1,), (0,))
NT = ((1,), (1,))
TN = ((0,), (0,))


def dot(a, b, dims):
    return lax.dot_general(a, b, (dims, ((), ())), preferred_element_type=F32)


def span(h):
    return slice(h * HEAD_DIM, (h + 1) * HEAD_DIM)


def causal_mask():
    rows = lax.broadcasted_iota(jnp.int32, (TOKENS, TOKENS), 0)
    cols = lax.broadcasted_iota(jnp.int32, (TOKENS, TOKENS), 1)
    return rows >= cols


def call(kernel, out, n_in, flops, any_in=0, scratch=(), any_out=False):
    vmem = pl.BlockSpec(memory_space=pltpu.VMEM)
    anys = pl.BlockSpec(memory_space=pl.ANY)
    return pl.pallas_call(
        kernel,
        out_shape=tuple(jax.ShapeDtypeStruct(s, d) for s, d in out),
        in_specs=[anys] * any_in + [vmem] * n_in,
        out_specs=tuple(anys if any_out else vmem for _ in out),
        scratch_shapes=scratch,
        compiler_params=pltpu.CompilerParams(vmem_limit_bytes=VMEM_LIMIT),
        cost_estimate=pl.CostEstimate(flops=flops, bytes_accessed=4 << 20, transcendentals=0),
    )


def state_kernel(k_ref, v_ref, w_ref, out_ref):
    for c in range(16):
        out_ref[c, 0:128] = w_ref[...]
        out_ref[c, 128:144, 256:] = jnp.zeros((16, 256), BF)
    for h in range(HEADS):
        state = dot(k_ref[:, span(h)], v_ref[:, span(h)], TN).astype(BF)
        for c in range(4):
            out_ref[4 * h + c, 128:144, 0:128] = state[32 * c : 32 * c + 16]
            out_ref[4 * h + c, 128:144, 128:256] = state[32 * c + 16 : 32 * c + 32]


def pick_kernel(in_ref, out_ref, part, sem):
    copy = pltpu.make_async_copy(in_ref.at[:, 128:144, 0:256], part, sem)
    copy.start()
    copy.wait()
    for c in range(16):
        out_ref[c, 0:16] = part[c, :, 0:128]
        out_ref[c, 16:32] = part[c, :, 128:256]


def scan_kernel(own_ref, other_ref, out_ref):
    second = when(lax.axis_index("core") == 1)
    run = jnp.zeros((32, HEAD_DIM), F32)
    for y in range(4):
        own = [own_ref[4 * y + x].astype(F32) for x in range(4)]
        others = sum(other_ref[4 * y + x].astype(F32) for x in range(4))
        before = run + others * second
        for x in range(4):
            out_ref[4 * y + x] = before.astype(BF)
            before = before + own[x]
        run = run + others + (own[0] + own[1] + own[2] + own[3])


def intra_kernel(q_ref, k_ref, v_ref, att_ref):
    mask = causal_mask()
    for h in range(HEADS):
        scores = dot(q_ref[:, span(h)], k_ref[:, span(h)], NT)
        scores = jnp.where(mask, scores, 0.0).astype(BF)
        att_ref[:, span(h)] = dot(scores, v_ref[:, span(h)], NN)


def when(flag):
    return jnp.where(flag, 1.0, 0.0).astype(F32)


def norm_kernel(q_ref, gain_ref, intra_ref, prior_ref, att_ref, gated_ref):
    for h in range(HEADS):
        rows = span(h)
        prior = prior_ref[rows]
        att = intra_ref[:, rows] + dot(q_ref[:, rows], prior, NN)
        att_ref[:, rows] = att
        inverse = lax.rsqrt(jnp.mean(att * att, axis=-1, keepdims=True) + EPS)
        gated = (att * inverse * gain_ref[:, rows]).astype(BF)
        gated_ref[rows, :] = gated.T


def halves(chunks):
    own, mate, f1, b1, f2, b2, f3, b3, f4, b4 = chunks

    def split(ref, k):
        return (ref.at[0:TOKENS], ref.at[TOKENS : 2 * TOKENS], k)

    same = [(own, mate, 0), split(f2, -2), split(b2, 2), (f4, b4, 4)]
    return same, [split(f1, -1), split(b1, 1), split(f3, -3), split(b3, 3)]


def by_parity(work, chunks):
    same = lax.rem(lax.axis_index("tp"), 2) == lax.axis_index("core")
    first, second = halves(chunks)
    pl.when(same)(lambda: work(first))
    pl.when(jnp.logical_not(same))(lambda: work(second))


def row_of(k):
    return lax.div(lax.rem(lax.axis_index("tp") + k + RING, RING), 2)


def main_kernel(*refs):
    chunks, rest = refs[:10], refs[10:]
    gated_ref, mate_ref, w_ref, near_ref, far_ref = rest[:5]
    own_ref, up_ref, down_ref, low_ref, high_ref, part_ref, acc = rest[5:]
    place = lax.axis_index("dp")

    def work(slots):
        for n, (near, far, k) in enumerate(slots):
            y = row_of(k)
            part = dot(gated_ref[...], near[...], NN) + dot(mate_ref[...], far[...], NN)
            part_ref[...] = part.astype(BF)
            blocks = []
            for d in range(4):
                start = pl.multiple_of(lax.rem(place + d, 4) * 128, 128)
                blocks.append(part_ref[:, pl.ds(start, 128)])
            own_ref[y], up_ref[y], down_ref[y] = blocks[0], blocks[1], blocks[3]
            low_ref[y], high_ref[y] = blocks[2][0:256], blocks[2][256:512]
            weight = w_ref[pl.ds(4 * y, 4), 0:128, :].reshape(WIDTH, WIDTH)
            part = dot(far[...], weight, NN)
            if n == 0:
                acc[...] = part
            elif n < 3:
                acc[...] += part
            else:
                far_ref[...] = (acc[...] + part).astype(BF)
            part = dot(near[...], weight, NN)
            near_ref[...] = part if n == 0 else near_ref[...] + part

    by_parity(work, chunks)


def tie(values, deps):
    def kernel(*refs):
        pass

    n = len(values)
    anys = pl.BlockSpec(memory_space=pl.ANY)
    return pl.pallas_call(
        kernel,
        out_shape=tuple(jax.ShapeDtypeStruct(v.shape, v.dtype) for v in values),
        in_specs=[anys] * (n + len(deps)),
        out_specs=(anys,) * n,
        input_output_aliases={i: i for i in range(n)},
        cost_estimate=pl.CostEstimate(flops=0, bytes_accessed=0, transcendentals=0),
    )(*values, *deps)


def relay_kernel(up_ref, down_ref, low_ref, high_ref, up_out, down_out):
    for y in range(4):
        up_out[y, 0:256] = (up_ref[y, 0:256].astype(F32) + low_ref[y].astype(F32)).astype(BF)
        up_out[y, 256:512] = up_ref[y, 256:512]
        down_out[y, 0:256] = down_ref[y, 0:256]
        low = down_ref[y, 256:512].astype(F32) + high_ref[y].astype(F32)
        down_out[y, 256:512] = low.astype(BF)


def column_kernel(own_ref, a_ref, b_ref, own_out, up_out, far_out, down_out):
    for e, out in enumerate((own_out, up_out, far_out, down_out)):
        y = lax.rem(lax.axis_index("y") + e, 4)
        total = own_ref[y].astype(F32) + a_ref[y].astype(F32) + b_ref[y].astype(F32)
        out[...] = total.astype(out.dtype)


def grad_kernel(own_ref, mate_ref, q_ref, att_ref, gain_ref, ga_ref, send_ref):
    base = HEADS * HEAD_DIM
    rows = lax.broadcasted_iota(jnp.int32, (16, HEAD_DIM), 0)
    sums = jnp.zeros((16, HEAD_DIM), F32)
    for h in range(HEADS):
        att = att_ref[:, span(h)]
        inverse = lax.rsqrt(jnp.mean(att * att, axis=-1, keepdims=True) + EPS)
        normed = att * inverse
        grad = own_ref[:, span(h)] + mate_ref[:, span(h)].astype(F32)
        part = jnp.sum(grad * normed, axis=0, keepdims=True)
        high = part.astype(BF).astype(F32)
        sums = sums + jnp.where(rows == h, high, 0.0) + jnp.where(rows == 4 + h, part - high, 0.0)
        grad = grad * gain_ref[:, span(h)]
        grad = (grad - normed * jnp.mean(grad * normed, axis=-1, keepdims=True)) * inverse
        grad = grad.astype(BF)
        ga_ref[:, span(h)] = grad
        send_ref[span(h)] = dot(q_ref[:, span(h)], grad, TN).astype(BF)
    send_ref[base:] = sums.astype(BF)


def resum(parts):
    total = sum(p.astype(F32) for p in parts)
    gain = total[0:4] + total[4:8]
    high = gain.astype(BF).astype(F32)
    return jnp.concatenate([high, gain - high, jnp.zeros((8, HEAD_DIM), F32)], axis=0)


def row_back_kernel(own_ref, r1_ref, r2_ref, r3_ref, total_ref, after_ref):
    x = lax.axis_index("dp")
    base = HEADS * HEAD_DIM
    r1, r2, r3 = (r[0:base].astype(F32) for r in (r1_ref, r2_ref, r3_ref))
    after_ref[...] = r1 * when(x <= 2) + r2 * when(x <= 1) + r3 * when(x <= 0)
    total_ref[0:base] = (own_ref[0:base].astype(F32) + r1 + r2 + r3).astype(BF)
    total_ref[base:] = resum([r[base:] for r in (own_ref, r1_ref, r2_ref, r3_ref)]).astype(BF)


def pair_back_kernel(total_ref, other_ref, out_ref):
    base = HEADS * HEAD_DIM
    out_ref[0:base] = (total_ref[0:base].astype(F32) + other_ref[0:base].astype(F32)).astype(BF)
    out_ref[base:] = resum([total_ref[base:], other_ref[base:]]).astype(BF)


def post_kernel(q_ref, k_ref, v_ref, ga_ref, prior_ref, qg_ref, kp_ref, vp_ref):
    mask = causal_mask()
    for h in range(HEADS):
        cols = span(h)
        q, k, v, ga = q_ref[:, cols], k_ref[:, cols], v_ref[:, cols], ga_ref[:, cols]
        scores = jnp.where(mask, dot(q, k, NT), 0.0).astype(BF)
        vp_ref[:, cols] = dot(scores, ga, TN)
        back = jnp.where(mask, dot(ga, v, NT), 0.0).astype(BF)
        qg_ref[:, cols] = (dot(back, k, NN) + dot(ga, prior_ref[cols], NT)).astype(BF)
        kp_ref[:, cols] = dot(back, q, TN)


def final_kernel(
    k_ref, v_ref, kp_ref, vp_ref, after_ref, other_ref, own, u1, u2, u3, kg_ref, vg_ref, gain_ref
):
    base = HEADS * HEAD_DIM
    y = lax.axis_index("y")
    first = when(lax.axis_index("core") == 0)
    for h in range(HEADS):
        cols = span(h)
        later = after_ref[cols] + other_ref[cols].astype(F32) * first
        later = later + u1[cols].astype(F32) * when(y <= 2) + u2[cols].astype(F32) * when(y <= 1)
        later = (later + u3[cols].astype(F32) * when(y <= 0)).astype(BF)
        kg_ref[:, cols] = (kp_ref[:, cols] + dot(v_ref[:, cols], later, NT)).astype(BF)
        vg_ref[:, cols] = (vp_ref[:, cols] + dot(k_ref[:, cols], later, NN)).astype(BF)
    gain_ref[...] = resum([r[base:] for r in (own, u1, u2, u3)]) * SCALE


def sum_kernel(own_ref, r1_ref, r2_ref, r3_ref, out_ref):
    total = own_ref[...]
    for ref in (r1_ref, r2_ref, r3_ref):
        total = total + ref[...].astype(F32)
    out_ref[...] = (total * SCALE).T


def shift(x, axis, size, k, wrap=True):
    pairs = [(i, (i + k) % size) for i in range(size) if wrap or 0 <= i + k < size]
    return lax.ppermute(x, axis, pairs)


def swap_cores(x):
    return lax.ppermute(x, "core", [(0, 1), (1, 0)])


def ring_step(x, parity, k):
    pairs = []
    for z in range(RING):
        core = (z + parity) % 2
        pairs.append((core * RING + z, core * RING + (z + k) % RING))
    return lax.ppermute(x, ("core", "tp"), pairs)


def body(queries, keys, values, gain, out_weight, out_cotangent):
    own = out_cotangent
    pairs = [((1 - z % 2) * RING + z, (z % 2) * RING + z) for z in range(RING)]
    mate = lax.ppermute(own, ("core", "tp"), pairs)
    chunks = [own, mate]
    fwd = bwd = jnp.concatenate([own, mate], axis=0)
    for step in range(2):
        fwd, bwd = ring_step(fwd, step, 1), ring_step(bwd, step, -1)
        chunks += [fwd, bwd]

    (spread,) = call(state_kernel, [((16, 144, WIDTH), BF)], 3, 1 << 27)(keys, values, out_weight)
    weight = lax.all_to_all(spread, PLANE, 0, 0, tiled=True)
    slices = ((16, 32, HEAD_DIM), BF)
    (states,) = call(
        pick_kernel,
        [slices],
        0,
        1 << 20,
        1,
        [pltpu.VMEM((16, 16, 256), BF), pltpu.SemaphoreType.DMA],
    )(weight)
    fwd, bwd = tie((fwd, bwd), (states,))
    chunks[4:6] = [fwd, bwd]
    fwd, bwd = ring_step(fwd, 0, 1), ring_step(bwd, 0, -1)
    chunks += [fwd, bwd, ring_step(fwd[:TOKENS], 1, 1), ring_step(bwd[TOKENS:], 1, -1)]
    (priors,) = call(scan_kernel, [slices], 2, 1 << 20)(states, swap_cores(states))
    prior = lax.all_to_all(priors, PLANE, 0, 0, tiled=True).reshape(STATE)
    (intra,) = call(intra_kernel, [(SQUARE, F32)], 3, 1 << 30)(queries, keys, values)
    gain_row = gain.reshape(1, WIDTH)
    att, gated = call(norm_kernel, [(SQUARE, F32), (SQUARE, BF)], 4, 1 << 28)(
        queries, gain_row, intra, prior
    )
    gated_mate = swap_cores(gated)

    quarter, eighth = ((4, WIDTH, 128), BF), ((4, WIDTH // 2, 128), BF)
    near, far, part, up, down, low, high = call(
        main_kernel,
        [(SQUARE, F32), (SQUARE, BF), quarter, quarter, quarter, eighth, eighth],
        13,
        1 << 33,
        0,
        [pltpu.VMEM(SQUARE, BF), pltpu.VMEM(SQUARE, F32)],
    )(*chunks, gated, gated_mate, weight)
    product_mate = swap_cores(far)
    up, down = call(relay_kernel, [quarter, quarter], 4, 1 << 20)(
        up, down, shift(low, "dp", 4, 1), shift(high, "dp", 4, -1)
    )
    block = (WIDTH, 128)
    part, up, away, down = call(
        column_kernel, [(block, F32), (block, BF), (block, BF), (block, BF)], 3, 1 << 20
    )(part, shift(up, "dp", 4, 1), shift(down, "dp", 4, -1))
    (weight_grad,) = call(sum_kernel, [((128, WIDTH), F32)], 4, 1 << 20)(
        part, shift(up, "y", 4, 1), shift(away, "y", 4, 2), shift(down, "y", 4, -1)
    )
    ga, send = call(grad_kernel, [(SQUARE, BF), (STATE_GAIN, BF)], 5, 1 << 29)(
        near, product_mate, queries, att, gain_row
    )
    total, after = call(row_back_kernel, [(STATE_GAIN, BF), (STATE, F32)], 4, 1 << 22)(
        send, *[shift(send, "dp", 4, -k) for k in (1, 2, 3)]
    )
    other = swap_cores(total)
    (both,) = call(pair_back_kernel, [(STATE_GAIN, BF)], 2, 1 << 22)(total, other)
    upper = [shift(both, "y", 4, -k) for k in (1, 2, 3)]
    query_grad, key_part, value_part = call(
        post_kernel, [(SQUARE, BF), (SQUARE, F32), (SQUARE, F32)], 5, 1 << 31
    )(queries, keys, values, ga, prior)
    key_grad, value_grad, gain_sum = call(
        final_kernel, [(SQUARE, BF), (SQUARE, BF), ((16, HEAD_DIM), F32)], 10, 1 << 28
    )(keys, values, key_part, value_part, after, other, both, *upper)
    gain_grad = (gain_sum[0:4] + gain_sum[4:8]).reshape(WIDTH)
    return query_grad, key_grad, value_grad, gain_grad, weight_grad


def solution(mesh):
    grid = Mesh(mesh.devices.reshape(4, 2, RING, 4), ("y", "core", "tp", "dp"))
    rows = P(("y", "core", "dp"), "tp")
    return jax.shard_map(
        body,
        mesh=grid,
        in_specs=(rows, rows, rows, P("tp"), rows, rows),
        out_specs=(rows, rows, rows, P("tp"), rows),
        check_vma=False,
    )
```

```python
import math

import jax
import jax.numpy as jnp
from jax import lax
from jax.experimental import pallas as pl
from jax.experimental.pallas import tpu as pltpu
from jax.sharding import Mesh
from jax.sharding import PartitionSpec as P

HEAD_DIM = 128
HEADS = 4
TOKENS = 512
WIDTH = 512
RING = 8
EPS = 1e-06
SCALE = 1.0 / math.sqrt(16384.0)
BF = jnp.bfloat16
F32 = jnp.float32
PLANE = ("y", "dp")
BLOCKS = ("y", "core", "dp")
VMEM_LIMIT = 24 * 1024 * 1024
STATE = (HEADS * HEAD_DIM, HEAD_DIM)
STATE_GAIN = (HEADS * HEAD_DIM + 16, HEAD_DIM)
SQUARE = (TOKENS, WIDTH)

NN = ((1,), (0,))
NT = ((1,), (1,))
TN = ((0,), (0,))


def dot(a, b, dims):
    return lax.dot_general(a, b, (dims, ((), ())), preferred_element_type=F32)


def span(h):
    return slice(h * HEAD_DIM, (h + 1) * HEAD_DIM)


def causal_mask():
    rows = lax.broadcasted_iota(jnp.int32, (TOKENS, TOKENS), 0)
    cols = lax.broadcasted_iota(jnp.int32, (TOKENS, TOKENS), 1)
    return rows >= cols


def call(kernel, out, n_in, flops, any_in=0, scratch=(), any_out=False):
    vmem = pl.BlockSpec(memory_space=pltpu.VMEM)
    anys = pl.BlockSpec(memory_space=pl.ANY)
    return pl.pallas_call(
        kernel,
        out_shape=tuple(jax.ShapeDtypeStruct(s, d) for s, d in out),
        in_specs=[anys] * any_in + [vmem] * n_in,
        out_specs=tuple(anys if any_out else vmem for _ in out),
        scratch_shapes=scratch,
        compiler_params=pltpu.CompilerParams(vmem_limit_bytes=VMEM_LIMIT),
        cost_estimate=pl.CostEstimate(flops=flops, bytes_accessed=4 << 20, transcendentals=0),
    )


def state_kernel(k_ref, v_ref, w_ref, out_ref, rows_ref):
    rows_ref[...] = w_ref[...]
    for h in range(HEADS):
        state = dot(k_ref[:, span(h)], v_ref[:, span(h)], TN).astype(BF)
        out_ref[h * 8 : (h + 1) * 8] = state.reshape(8, 16, HEAD_DIM)


def scan_kernel(in_ref, out_ref):
    total = jnp.zeros((16, HEAD_DIM), F32)
    for c in range(32):
        out_ref[c] = total.astype(BF)
        total = total + in_ref[c].astype(F32)


def intra_kernel(q_ref, k_ref, v_ref, att_ref):
    mask = causal_mask()
    for h in range(HEADS):
        scores = dot(q_ref[:, span(h)], k_ref[:, span(h)], NT)
        scores = jnp.where(mask, scores, 0.0).astype(BF)
        att_ref[:, span(h)] = dot(scores, v_ref[:, span(h)], NN)


def when(flag):
    return jnp.where(flag, 1.0, 0.0).astype(F32)


def norm_kernel(q_ref, gain_ref, intra_ref, prior_ref, att_ref, gated_ref):
    for h in range(HEADS):
        rows = span(h)
        prior = prior_ref[rows]
        att = intra_ref[:, rows] + dot(q_ref[:, rows], prior, NN)
        att_ref[:, rows] = att
        inverse = lax.rsqrt(jnp.mean(att * att, axis=-1, keepdims=True) + EPS)
        gated = (att * inverse * gain_ref[:, rows]).astype(BF)
        gated_ref[rows, :] = gated.T


def is_same():
    return lax.rem(lax.axis_index("tp"), 2) == lax.axis_index("core")


def row_of(k):
    return lax.div(lax.rem(lax.axis_index("tp") + k + RING, RING), 2)


EVENS = (0, 2, -2, 4)
ODDS = (1, -1, 3, -3)


def early_kernel(after1_ref, after2_ref, *refs):
    own, f1, b1, f2, b2, f3, b3, gated_ref, wm_ref, wo_ref = refs[:10]
    sum_ref, mine_ref, other_ref, block_ref, weight_ref = refs[10:]

    def weight_of(w_ref, k):
        return w_ref[row_of(k)].reshape(WIDTH, WIDTH)

    def work(w_even, out_even, w_odd, out_odd):
        first = True
        for rows, w_ref, out, ks in (
            ((own, b2, f2), w_even, out_even, EVENS),
            ((b1, f1, b3), w_odd, out_odd, ODDS),
        ):
            for s, ref in enumerate(rows):
                out[s] = dot(gated_ref[...], ref[...], NN).astype(BF)
                part = dot(ref[...], weight_of(w_ref, ks[s]), NN)
                sum_ref[...] = part if first else sum_ref[...] + part
                first = False
        block_ref[...] = dot(gated_ref[...], f3[...], NN).astype(BF)
        sum_ref[...] += dot(f3[...], weight_of(w_odd, -3), NN)
        weight_ref[...] = weight_of(w_even, 4)

    pl.when(is_same())(lambda: work(wm_ref, mine_ref, wo_ref, other_ref))
    pl.when(jnp.logical_not(is_same()))(lambda: work(wo_ref, other_ref, wm_ref, mine_ref))


def late_kernel(
    low_ref, high_ref, gated_ref, block_ref, weight_ref, sum_ref, q_ref, att_ref, gain_ref,
    ga_ref, send_ref, mine_ref, other_ref, acc,
):
    half = TOKENS // 2
    last = dot(gated_ref[:, 0:half], low_ref[...], NN)
    last = (last + dot(gated_ref[:, half:TOKENS], high_ref[...], NN)).astype(BF)

    @pl.when(is_same())
    def _():
        mine_ref[...] = last
        other_ref[...] = block_ref[...]

    @pl.when(jnp.logical_not(is_same()))
    def _():
        mine_ref[...] = block_ref[...]
        other_ref[...] = last

    acc[0:half] = sum_ref[0:half] + dot(low_ref[...], weight_ref[...], NN)
    acc[half:TOKENS] = sum_ref[half:TOKENS] + dot(high_ref[...], weight_ref[...], NN)
    grad_rows(acc, q_ref, att_ref, gain_ref, ga_ref, send_ref)


def combine_kernel(
    mine_ref, got_ref, mine_last, got_last,
    own_ref, up_ref, down_ref, low_ref, high_ref, part_ref,
):
    place = lax.axis_index("dp")
    for s in range(4):
        mine, got = (mine_ref[s], got_ref[s]) if s < 3 else (mine_last[...], got_last[...])
        part_ref[...] = (mine.astype(F32) + got.astype(F32)).astype(BF)
        blocks = []
        for d in range(4):
            start = pl.multiple_of(lax.rem(place + d, 4) * 128, 128)
            blocks.append(part_ref[:, pl.ds(start, 128)])
        own_ref[s], up_ref[s], down_ref[s] = blocks[0], blocks[1], blocks[3]
        low_ref[s * 256 : (s + 1) * 256] = blocks[2][0:256]
        high_ref[s * 256 : (s + 1) * 256] = blocks[2][256:512]


def pack_kernel(after1_ref, after2_ref, own_ref, r1_ref, r2_ref, r3_ref, out_ref):
    y = lax.axis_index("y")
    for k, ref in enumerate((own_ref, r1_ref, r2_ref, r3_ref)):
        out_ref[lax.rem(y + 4 - k, 4)] = ref[...]


def relay_rows_kernel(after1_ref, after2_ref, low_ref, high_ref, low_out, high_out):
    low_out[...] = low_ref[0:2]
    high_out[...] = high_ref[2:4]


def turn_kernel(
    after_ref, fwd_ref, bwd_ref, own_ref, low_ref, high_ref, far_low_ref, far_high_ref,
    fwd_out, bwd_out, out_ref,
):
    fwd_out[...] = fwd_ref[0 : TOKENS // 2]
    bwd_out[...] = bwd_ref[TOKENS // 2 : TOKENS]
    x = lax.axis_index("dp")
    for k, ref in ((0, own_ref), (3, low_ref), (1, high_ref)):
        for y in range(4):
            out_ref[y, lax.rem(x + k, 4)] = ref[y]
    for y in range(2):
        out_ref[y, lax.rem(x + 2, 4)] = far_low_ref[y]
        out_ref[2 + y, lax.rem(x + 2, 4)] = far_high_ref[y]


def tie(values, deps):
    def kernel(*refs):
        pass

    n = len(values)
    anys = pl.BlockSpec(memory_space=pl.ANY)
    return pl.pallas_call(
        kernel,
        out_shape=tuple(jax.ShapeDtypeStruct(v.shape, v.dtype) for v in values),
        in_specs=[anys] * (n + len(deps)),
        out_specs=(anys,) * n,
        input_output_aliases={i: i for i in range(n)},
        cost_estimate=pl.CostEstimate(flops=0, bytes_accessed=0, transcendentals=0),
    )(*values, *deps)


def relay_kernel(after_ref, up_ref, down_ref, low_ref, high_ref, up_out, down_out):
    for y in range(4):
        rows = slice(y * 256, (y + 1) * 256)
        up_out[y, 0:256] = (up_ref[y, 0:256].astype(F32) + low_ref[rows].astype(F32)).astype(BF)
        up_out[y, 256:512] = up_ref[y, 256:512]
        down_out[y, 0:256] = down_ref[y, 0:256]
        low = down_ref[y, 256:512].astype(F32) + high_ref[rows].astype(F32)
        down_out[y, 256:512] = low.astype(BF)


def column_kernel(own_ref, a_ref, b_ref, own_out, up_out, far_out, down_out, rows):
    for s in range(4):
        y = row_of(jnp.where(is_same(), EVENS[s], ODDS[s]))
        total = own_ref[s].astype(F32) + a_ref[s].astype(F32) + b_ref[s].astype(F32)
        rows[lax.rem(y + 4 - lax.axis_index("y"), 4)] = total
    own_out[...] = rows[0]
    up_out[...] = rows[1].astype(BF)
    far_out[...] = rows[2].astype(BF)
    down_out[...] = rows[3].astype(BF)


def grad_rows(own_ref, q_ref, att_ref, gain_ref, ga_ref, send_ref):
    base = HEADS * HEAD_DIM
    rows = lax.broadcasted_iota(jnp.int32, (16, HEAD_DIM), 0)
    sums = jnp.zeros((16, HEAD_DIM), F32)
    for h in range(HEADS):
        att = att_ref[:, span(h)]
        inverse = lax.rsqrt(jnp.mean(att * att, axis=-1, keepdims=True) + EPS)
        normed = att * inverse
        grad = own_ref[:, span(h)]
        part = jnp.sum(grad * normed, axis=0, keepdims=True)
        high = part.astype(BF).astype(F32)
        sums = sums + jnp.where(rows == h, high, 0.0) + jnp.where(rows == 4 + h, part - high, 0.0)
        grad = grad * gain_ref[:, span(h)]
        grad = (grad - normed * jnp.mean(grad * normed, axis=-1, keepdims=True)) * inverse
        grad = grad.astype(BF)
        ga_ref[:, span(h)] = grad
        send_ref[span(h)] = dot(q_ref[:, span(h)], grad, TN).astype(BF)
    send_ref[base:] = sums.astype(BF)


def resum(parts):
    total = sum(p.astype(F32) for p in parts)
    gain = total[0:4] + total[4:8]
    high = gain.astype(BF).astype(F32)
    return jnp.concatenate([high, gain - high, jnp.zeros((8, HEAD_DIM), F32)], axis=0)


def row_back_kernel(own_ref, r1_ref, r2_ref, r3_ref, total_ref, after_ref):
    x = lax.axis_index("dp")
    base = HEADS * HEAD_DIM
    r1, r2, r3 = (r[0:base].astype(F32) for r in (r1_ref, r2_ref, r3_ref))
    after_ref[...] = r1 * when(x <= 2) + r2 * when(x <= 1) + r3 * when(x <= 0)
    total_ref[0:base] = (own_ref[0:base].astype(F32) + r1 + r2 + r3).astype(BF)
    total_ref[base:] = resum([r[base:] for r in (own_ref, r1_ref, r2_ref, r3_ref)]).astype(BF)


def pair_back_kernel(total_ref, other_ref, out_ref):
    base = HEADS * HEAD_DIM
    out_ref[0:base] = (total_ref[0:base].astype(F32) + other_ref[0:base].astype(F32)).astype(BF)
    out_ref[base:] = resum([total_ref[base:], other_ref[base:]]).astype(BF)


def post_kernel(q_ref, k_ref, v_ref, ga_ref, prior_ref, qg_ref, kp_ref, vp_ref):
    mask = causal_mask()
    for h in range(HEADS):
        cols = span(h)
        q, k, v, ga = q_ref[:, cols], k_ref[:, cols], v_ref[:, cols], ga_ref[:, cols]
        scores = jnp.where(mask, dot(q, k, NT), 0.0).astype(BF)
        vp_ref[:, cols] = dot(scores, ga, TN)
        back = jnp.where(mask, dot(ga, v, NT), 0.0).astype(BF)
        qg_ref[:, cols] = (dot(back, k, NN) + dot(ga, prior_ref[cols], NT)).astype(BF)
        kp_ref[:, cols] = dot(back, q, TN)


def final_kernel(
    k_ref, v_ref, kp_ref, vp_ref, after_ref, other_ref, own, u1, u2, u3, kg_ref, vg_ref, gain_ref
):
    base = HEADS * HEAD_DIM
    y = lax.axis_index("y")
    first = when(lax.axis_index("core") == 0)
    for h in range(HEADS):
        cols = span(h)
        later = after_ref[cols] + other_ref[cols].astype(F32) * first
        later = later + u1[cols].astype(F32) * when(y <= 2) + u2[cols].astype(F32) * when(y <= 1)
        later = (later + u3[cols].astype(F32) * when(y <= 0)).astype(BF)
        kg_ref[:, cols] = (kp_ref[:, cols] + dot(v_ref[:, cols], later, NT)).astype(BF)
        vg_ref[:, cols] = (vp_ref[:, cols] + dot(k_ref[:, cols], later, NN)).astype(BF)
    gain_ref[...] = resum([r[base:] for r in (own, u1, u2, u3)]) * SCALE


def sum_kernel(own_ref, r1_ref, r2_ref, r3_ref, out_ref):
    total = own_ref[...]
    for ref in (r1_ref, r2_ref, r3_ref):
        total = total + ref[...].astype(F32)
    out_ref[...] = (total * SCALE).T


def shift(x, axis, size, k, wrap=True):
    pairs = [(i, (i + k) % size) for i in range(size) if wrap or 0 <= i + k < size]
    return lax.ppermute(x, axis, pairs)


def swap_cores(x):
    return lax.ppermute(x, "core", [(0, 1), (1, 0)])


def body(queries, keys, values, gain, out_weight, out_cotangent):
    own = out_cotangent
    fwd, bwd = shift(own, "tp", RING, 1), shift(own, "tp", RING, -1)
    slices = ((32, 16, HEAD_DIM), BF)
    state, rows = call(state_kernel, [slices, ((128, WIDTH), BF)], 3, 1 << 27)(
        keys, values, out_weight
    )
    states = lax.all_to_all(state, BLOCKS, 0, 0, tiled=True)
    others = [shift(rows, "y", 4, k) for k in (1, 2, 3)]
    (column,) = call(pack_kernel, [((4, 128, WIDTH), BF)], 4, 1 << 20, 2)(fwd, bwd, rows, *others)
    fwd, bwd = tie((fwd, bwd), (states, column))
    chunks = [own, fwd, bwd]

    fwd, bwd = shift(fwd, "tp", RING, 1), shift(bwd, "tp", RING, -1)
    (priors,) = call(scan_kernel, [slices], 1, 1 << 20)(states)
    prior = lax.all_to_all(priors, BLOCKS, 0, 0, tiled=True).reshape(STATE)
    column_low, column_high = shift(column, "dp", 4, 1), shift(column, "dp", 4, -1)
    (intra,) = call(intra_kernel, [(SQUARE, F32)], 3, 1 << 30)(queries, keys, values)
    gain_row = gain.reshape(1, WIDTH)
    att, gated = call(norm_kernel, [(SQUARE, F32), (SQUARE, BF)], 4, 1 << 28)(
        queries, gain_row, intra, prior
    )
    relay = ((2, 128, WIDTH), BF)
    relay_low, relay_high = call(relay_rows_kernel, [relay, relay], 2, 0, 2)(
        fwd, bwd, column_low, column_high
    )
    fwd, bwd = tie((fwd, bwd), (relay_low, relay_high))
    chunks += [fwd, bwd]

    fwd, bwd = shift(fwd, "tp", RING, 1), shift(bwd, "tp", RING, -1)
    relay_low, relay_high = shift(relay_low, "dp", 4, 1), shift(relay_high, "dp", 4, -1)
    half = ((TOKENS // 2, WIDTH), BF)
    last_low, last_high, weight = call(
        turn_kernel, [half, half, ((4, 4, 128, WIDTH), BF)], 7, 1 << 20, 1
    )(gated, fwd, bwd, column, column_low, column_high, relay_low, relay_high)
    chunks += [fwd, bwd]
    last_low, last_high = shift(last_low, "tp", RING, 1), shift(last_high, "tp", RING, -1)
    weight_other = swap_cores(weight)

    wide = ((3, WIDTH, WIDTH), BF)
    partial_sum, mine, other, block, weight_last = call(
        early_kernel, [(SQUARE, F32), wide, wide, (SQUARE, BF), (SQUARE, BF)], 10, 1 << 33, 2
    )(last_low, last_high, *chunks, gated, weight, weight_other)
    other = swap_cores(other)
    ga, send, mine_last, other_last = call(
        late_kernel,
        [(SQUARE, BF), (STATE_GAIN, BF), (SQUARE, BF), (SQUARE, BF)],
        9,
        1 << 31,
        0,
        [pltpu.VMEM(SQUARE, F32)],
    )(last_low, last_high, gated, block, weight_last, partial_sum, queries, att, gain_row)
    quarter, eighth = ((4, WIDTH, 128), BF), ((2 * WIDTH, 128), BF)
    part, up, down, low, high = call(
        combine_kernel,
        [quarter, quarter, quarter, eighth, eighth],
        4,
        1 << 20,
        0,
        [pltpu.VMEM(SQUARE, BF)],
    )(mine, other, mine_last, swap_cores(other_last))
    total, after = call(row_back_kernel, [(STATE_GAIN, BF), (STATE, F32)], 4, 1 << 22)(
        send, *[shift(send, "dp", 4, -k) for k in (1, 2, 3)]
    )
    up, down = call(relay_kernel, [quarter, quarter], 4, 1 << 20, 1)(
        total, up, down, shift(low, "dp", 4, 1), shift(high, "dp", 4, -1)
    )
    block = (WIDTH, 128)
    part, up, away, down = call(
        column_kernel,
        [(block, F32), (block, BF), (block, BF), (block, BF)],
        3,
        1 << 20,
        0,
        [pltpu.VMEM((4, WIDTH, 128), F32)],
    )(part, shift(up, "dp", 4, 1), shift(down, "dp", 4, -1))
    (weight_grad,) = call(sum_kernel, [((128, WIDTH), F32)], 4, 1 << 20)(
        part, shift(up, "y", 4, 1), shift(away, "y", 4, 2), shift(down, "y", 4, -1)
    )
    other = swap_cores(total)
    (both,) = call(pair_back_kernel, [(STATE_GAIN, BF)], 2, 1 << 22)(total, other)
    upper = [shift(both, "y", 4, -k) for k in (1, 2, 3)]
    query_grad, key_part, value_part = call(
        post_kernel, [(SQUARE, BF), (SQUARE, F32), (SQUARE, F32)], 5, 1 << 31
    )(queries, keys, values, ga, prior)
    key_grad, value_grad, gain_sum = call(
        final_kernel, [(SQUARE, BF), (SQUARE, BF), ((16, HEAD_DIM), F32)], 10, 1 << 28
    )(keys, values, key_part, value_part, after, other, both, *upper)
    gain_grad = (gain_sum[0:4] + gain_sum[4:8]).reshape(WIDTH)
    return query_grad, key_grad, value_grad, gain_grad, weight_grad


def solution(mesh):
    grid = Mesh(mesh.devices.reshape(4, 2, RING, 4), ("y", "core", "tp", "dp"))
    rows = P(("y", "core", "dp"), "tp")
    return jax.shard_map(
        body,
        mesh=grid,
        in_specs=(rows, rows, rows, P("tp"), rows, rows),
        out_specs=(rows, rows, rows, P("tp"), rows),
        check_vma=False,
    )
```

```python
import math

import jax
import jax.numpy as jnp
from jax import lax
from jax.experimental import pallas as pl
from jax.experimental.pallas import tpu as pltpu
from jax.sharding import Mesh
from jax.sharding import PartitionSpec as P

HEAD_DIM = 128
HEADS = 4
TOKENS = 512
WIDTH = 512
RING = 8
EPS = 1e-06
SCALE = 1.0 / math.sqrt(16384.0)
BF = jnp.bfloat16
F32 = jnp.float32
PLANE = ("y", "dp")
BLOCKS = ("y", "core", "dp")
VMEM_LIMIT = 24 * 1024 * 1024
STATE = (HEADS * HEAD_DIM, HEAD_DIM)
STATE_GAIN = (HEADS * HEAD_DIM + 16, HEAD_DIM)
SQUARE = (TOKENS, WIDTH)
TOKEN = ((8, HEAD_DIM), jnp.float32)

NN = ((1,), (0,))
NT = ((1,), (1,))
TN = ((0,), (0,))


def dot(a, b, dims):
    return lax.dot_general(a, b, (dims, ((), ())), preferred_element_type=F32)


def span(h):
    return slice(h * HEAD_DIM, (h + 1) * HEAD_DIM)


def causal_mask():
    rows = lax.broadcasted_iota(jnp.int32, (TOKENS, TOKENS), 0)
    cols = lax.broadcasted_iota(jnp.int32, (TOKENS, TOKENS), 1)
    return rows >= cols


def call(kernel, out, n_in, flops, any_in=0, scratch=(), any_out=False):
    vmem = pl.BlockSpec(memory_space=pltpu.VMEM)
    anys = pl.BlockSpec(memory_space=pl.ANY)
    return pl.pallas_call(
        kernel,
        out_shape=tuple(jax.ShapeDtypeStruct(s, d) for s, d in out),
        in_specs=[anys] * any_in + [vmem] * n_in,
        out_specs=tuple(anys if any_out else vmem for _ in out),
        scratch_shapes=scratch,
        compiler_params=pltpu.CompilerParams(vmem_limit_bytes=VMEM_LIMIT),
        cost_estimate=pl.CostEstimate(flops=flops, bytes_accessed=4 << 20, transcendentals=0),
    )


def state_kernel(k_ref, v_ref, out_ref, token_ref):
    token_ref[...] = jnp.zeros(TOKEN[0], F32)
    for h in range(HEADS):
        state = dot(k_ref[:, span(h)], v_ref[:, span(h)], TN).astype(BF)
        out_ref[h * 8 : (h + 1) * 8] = state.reshape(8, 16, HEAD_DIM)


def scan_kernel(in_ref, out_ref, token_ref):
    token_ref[...] = jnp.zeros(TOKEN[0], F32)
    total = jnp.zeros((16, HEAD_DIM), F32)
    for c in range(32):
        out_ref[c] = total.astype(BF)
        total = total + in_ref[c].astype(F32)


def when(flag):
    return jnp.where(flag, 1.0, 0.0).astype(F32)


def norm_kernel(q_ref, k_ref, v_ref, gain_ref, prior_ref, att_ref, gated_ref):
    mask = causal_mask()
    for h in range(HEADS):
        rows = span(h)
        scores = dot(q_ref[:, rows], k_ref[:, rows], NT)
        scores = jnp.where(mask, scores, 0.0).astype(BF)
        att = dot(scores, v_ref[:, rows], NN) + dot(q_ref[:, rows], prior_ref[rows], NN)
        att_ref[:, rows] = att
        inverse = lax.rsqrt(jnp.mean(att * att, axis=-1, keepdims=True) + EPS)
        gated = (att * inverse * gain_ref[:, rows]).astype(BF)
        gated_ref[rows, :] = gated.T


def is_same():
    return lax.rem(lax.axis_index("tp"), 2) == lax.axis_index("core")


def row_of(k):
    return lax.div(lax.rem(lax.axis_index("tp") + k + RING, RING), 2)


EVENS = (0, 2, -2, 4)
ODDS = (1, -1, 3, -3)


def early_kernel(*refs):
    own, f1, b1, f2, b2, f3, b3, gated_ref, wm_ref, wo_ref = refs[:10]
    sum_ref, mine_ref, other_ref, block_ref, weight_ref = refs[10:]

    def weight_of(w_ref, k):
        return w_ref[row_of(k)].reshape(WIDTH, WIDTH)

    def work(w_even, out_even, w_odd, out_odd):
        first = True
        for rows, w_ref, out, ks in (
            ((own, b2, f2), w_even, out_even, EVENS),
            ((b1, f1, b3), w_odd, out_odd, ODDS),
        ):
            for s, ref in enumerate(rows):
                out[s] = dot(gated_ref[...], ref[...], NN).astype(BF)
                part = dot(ref[...], weight_of(w_ref, ks[s]), NN)
                sum_ref[...] = part if first else sum_ref[...] + part
                first = False
        block_ref[...] = dot(gated_ref[...], f3[...], NN).astype(BF)
        sum_ref[...] += dot(f3[...], weight_of(w_odd, -3), NN)
        weight_ref[...] = weight_of(w_even, 4)

    pl.when(is_same())(lambda: work(wm_ref, mine_ref, wo_ref, other_ref))
    pl.when(jnp.logical_not(is_same()))(lambda: work(wo_ref, other_ref, wm_ref, mine_ref))


def late_kernel(
    low_ref, high_ref, gated_ref, block_ref, weight_ref, sum_ref, q_ref, att_ref, gain_ref,
    early_ref, ga_ref, send_ref, mine_ref, other_ref, acc,
):
    half = TOKENS // 2
    last = dot(gated_ref[:, 0:half], low_ref[...], NN)
    last = (last + dot(gated_ref[:, half:TOKENS], high_ref[...], NN)).astype(BF)

    @pl.when(is_same())
    def _():
        mine_ref[...] = last
        other_ref[3] = block_ref[...]

    @pl.when(jnp.logical_not(is_same()))
    def _():
        mine_ref[...] = block_ref[...]
        other_ref[3] = last

    acc[0:half] = sum_ref[0:half] + dot(low_ref[...], weight_ref[...], NN)
    acc[half:TOKENS] = sum_ref[half:TOKENS] + dot(high_ref[...], weight_ref[...], NN)
    grad_rows(acc, q_ref, att_ref, gain_ref, ga_ref, send_ref)
    other_ref[0:3] = early_ref[...]


def combine_kernel(
    mine_ref, got_ref, mine_last,
    own_ref, up_ref, down_ref, low_ref, high_ref, part_ref,
):
    place = lax.axis_index("dp")
    for s in range(4):
        mine, got = mine_ref[s] if s < 3 else mine_last[...], got_ref[s]
        part_ref[...] = (mine.astype(F32) + got.astype(F32)).astype(BF)
        blocks = []
        for d in range(4):
            start = pl.multiple_of(lax.rem(place + d, 4) * 128, 128)
            blocks.append(part_ref[:, pl.ds(start, 128)])
        own_ref[s], up_ref[s], down_ref[s] = blocks[0], blocks[1], blocks[3]
        low_ref[s * 256 : (s + 1) * 256] = blocks[2][0:256]
        high_ref[s * 256 : (s + 1) * 256] = blocks[2][256:512]


def pack_kernel(after1_ref, after2_ref, own_ref, r1_ref, r2_ref, r3_ref, out_ref, token_ref):
    token_ref[...] = jnp.zeros(TOKEN[0], F32)
    y = lax.axis_index("y")
    for k, ref in enumerate((own_ref, r1_ref, r2_ref, r3_ref)):
        out_ref[lax.rem(y + 4 - k, 4)] = ref[...]


def relay_rows_kernel(after1_ref, after2_ref, low_ref, high_ref, low_out, high_out, sems):
    low = pltpu.make_async_copy(low_ref.at[0:2], low_out, sems.at[0])
    high = pltpu.make_async_copy(high_ref.at[2:4], high_out, sems.at[1])
    low.start()
    high.start()
    low.wait()
    high.wait()


def turn_kernel(
    after_ref, fwd_ref, bwd_ref, own_ref, low_ref, high_ref, far_low_ref, far_high_ref,
    fwd_out, bwd_out, out_ref,
):
    fwd_out[...] = fwd_ref[0 : TOKENS // 2]
    bwd_out[...] = bwd_ref[TOKENS // 2 : TOKENS]
    x = lax.axis_index("dp")
    for k, ref in ((0, own_ref), (3, low_ref), (1, high_ref)):
        for y in range(4):
            out_ref[y, lax.rem(x + k, 4)] = ref[y]
    for y in range(2):
        out_ref[y, lax.rem(x + 2, 4)] = far_low_ref[y]
        out_ref[2 + y, lax.rem(x + 2, 4)] = far_high_ref[y]


def tie(values, deps):
    def kernel(*refs):
        pass

    n = len(values)
    anys = pl.BlockSpec(memory_space=pl.ANY)
    vmem = pl.BlockSpec(memory_space=pltpu.VMEM)
    return pl.pallas_call(
        kernel,
        out_shape=tuple(jax.ShapeDtypeStruct(v.shape, v.dtype) for v in values),
        in_specs=[anys] * n + [vmem] * len(deps),
        out_specs=(anys,) * n,
        input_output_aliases={i: i for i in range(n)},
        cost_estimate=pl.CostEstimate(flops=0, bytes_accessed=0, transcendentals=0),
    )(*values, *deps)


def relay_kernel(after_ref, up_ref, down_ref, low_ref, high_ref, up_out, down_out):
    for y in range(4):
        rows = slice(y * 256, (y + 1) * 256)
        up_out[y, 0:256] = (up_ref[y, 0:256].astype(F32) + low_ref[rows].astype(F32)).astype(BF)
        up_out[y, 256:512] = up_ref[y, 256:512]
        down_out[y, 0:256] = down_ref[y, 0:256]
        low = down_ref[y, 256:512].astype(F32) + high_ref[rows].astype(F32)
        down_out[y, 256:512] = low.astype(BF)


def column_kernel(own_ref, a_ref, b_ref, own_out, up_out, far_out, down_out, rows):
    for s in range(4):
        y = row_of(jnp.where(is_same(), EVENS[s], ODDS[s]))
        total = own_ref[s].astype(F32) + a_ref[s].astype(F32) + b_ref[s].astype(F32)
        rows[lax.rem(y + 4 - lax.axis_index("y"), 4)] = total
    own_out[...] = rows[0]
    up_out[...] = rows[1].astype(BF)
    far_out[...] = rows[2].astype(BF)
    down_out[...] = rows[3].astype(BF)


def grad_rows(own_ref, q_ref, att_ref, gain_ref, ga_ref, send_ref):
    base = HEADS * HEAD_DIM
    rows = lax.broadcasted_iota(jnp.int32, (16, HEAD_DIM), 0)
    sums = jnp.zeros((16, HEAD_DIM), F32)
    for h in range(HEADS):
        att = att_ref[:, span(h)]
        inverse = lax.rsqrt(jnp.mean(att * att, axis=-1, keepdims=True) + EPS)
        normed = att * inverse
        grad = own_ref[:, span(h)]
        part = jnp.sum(grad * normed, axis=0, keepdims=True)
        high = part.astype(BF).astype(F32)
        sums = sums + jnp.where(rows == h, high, 0.0) + jnp.where(rows == 4 + h, part - high, 0.0)
        grad = grad * gain_ref[:, span(h)]
        grad = (grad - normed * jnp.mean(grad * normed, axis=-1, keepdims=True)) * inverse
        grad = grad.astype(BF)
        ga_ref[:, span(h)] = grad
        send_ref[span(h)] = dot(q_ref[:, span(h)], grad, TN).astype(BF)
    send_ref[base:] = sums.astype(BF)


def resum(parts):
    total = sum(p.astype(F32) for p in parts)
    gain = total[0:4] + total[4:8]
    high = gain.astype(BF).astype(F32)
    return jnp.concatenate([high, gain - high, jnp.zeros((8, HEAD_DIM), F32)], axis=0)


def row_back_kernel(own_ref, r1_ref, r2_ref, r3_ref, total_ref, after_ref):
    x = lax.axis_index("dp")
    base = HEADS * HEAD_DIM
    r1, r2, r3 = (r[0:base].astype(F32) for r in (r1_ref, r2_ref, r3_ref))
    after_ref[...] = r1 * when(x <= 2) + r2 * when(x <= 1) + r3 * when(x <= 0)
    total_ref[0:base] = (own_ref[0:base].astype(F32) + r1 + r2 + r3).astype(BF)
    total_ref[base:] = resum([r[base:] for r in (own_ref, r1_ref, r2_ref, r3_ref)]).astype(BF)


def pair_back_kernel(total_ref, other_ref, out_ref):
    base = HEADS * HEAD_DIM
    out_ref[0:base] = (total_ref[0:base].astype(F32) + other_ref[0:base].astype(F32)).astype(BF)
    out_ref[base:] = resum([total_ref[base:], other_ref[base:]]).astype(BF)


def post_kernel(q_ref, k_ref, v_ref, ga_ref, prior_ref, qg_ref, kp_ref, vp_ref):
    mask = causal_mask()
    for h in range(HEADS):
        cols = span(h)
        q, k, v, ga = q_ref[:, cols], k_ref[:, cols], v_ref[:, cols], ga_ref[:, cols]
        scores = jnp.where(mask, dot(q, k, NT), 0.0).astype(BF)
        vp_ref[:, cols] = dot(scores, ga, TN)
        back = jnp.where(mask, dot(ga, v, NT), 0.0).astype(BF)
        qg_ref[:, cols] = (dot(back, k, NN) + dot(ga, prior_ref[cols], NT)).astype(BF)
        kp_ref[:, cols] = dot(back, q, TN)


def final_kernel(
    after_last_ref, k_ref, v_ref, kp_ref, vp_ref, after_ref, other_ref, own, u1, u2, u3, kg_ref, vg_ref, gain_ref
):
    base = HEADS * HEAD_DIM
    y = lax.axis_index("y")
    first = when(lax.axis_index("core") == 0)
    for h in range(HEADS):
        cols = span(h)
        later = after_ref[cols] + other_ref[cols].astype(F32) * first
        later = later + u1[cols].astype(F32) * when(y <= 2) + u2[cols].astype(F32) * when(y <= 1)
        later = (later + u3[cols].astype(F32) * when(y <= 0)).astype(BF)
        kg_ref[:, cols] = (kp_ref[:, cols] + dot(v_ref[:, cols], later, NT)).astype(BF)
        vg_ref[:, cols] = (vp_ref[:, cols] + dot(k_ref[:, cols], later, NN)).astype(BF)
    gain_ref[...] = resum([r[base:] for r in (own, u1, u2, u3)]) * SCALE


def sum_kernel(own_ref, r1_ref, r2_ref, r3_ref, out_ref):
    total = own_ref[...]
    for ref in (r1_ref, r2_ref, r3_ref):
        total = total + ref[...].astype(F32)
    out_ref[...] = (total * SCALE).T


def shift(x, axis, size, k, wrap=True):
    pairs = [(i, (i + k) % size) for i in range(size) if wrap or 0 <= i + k < size]
    return lax.ppermute(x, axis, pairs)


def swap_cores(x):
    return lax.ppermute(x, "core", [(0, 1), (1, 0)])


def body(queries, keys, values, gain, out_weight, out_cotangent):
    own = out_cotangent
    fwd, bwd = shift(own, "tp", RING, 1), shift(own, "tp", RING, -1)
    slices = ((32, 16, HEAD_DIM), BF)
    state, state_token = call(state_kernel, [slices, TOKEN], 2, 1 << 27)(keys, values)
    states = lax.all_to_all(state, BLOCKS, 0, 0, tiled=True)
    others = [shift(out_weight, "y", 4, k) for k in (1, 2, 3)]
    column, column_token = call(pack_kernel, [((4, 128, WIDTH), BF), TOKEN], 4, 1 << 20, 2)(
        fwd, bwd, out_weight, *others
    )
    fwd, bwd = tie((fwd, bwd), (state_token, column_token))
    chunks = [own, fwd, bwd]

    fwd, bwd = shift(fwd, "tp", RING, 1), shift(bwd, "tp", RING, -1)
    priors, scan_token = call(scan_kernel, [slices, TOKEN], 1, 1 << 20)(states)
    prior = lax.all_to_all(priors, BLOCKS, 0, 0, tiled=True).reshape(STATE)
    column_low, column_high = shift(column, "dp", 4, 1), shift(column, "dp", 4, -1)
    gain_row = gain.reshape(1, WIDTH)
    att, gated = call(norm_kernel, [(SQUARE, F32), (SQUARE, BF)], 5, 1 << 30)(
        queries, keys, values, gain_row, prior
    )
    relay = ((2, 128, WIDTH), BF)
    relay_low, relay_high = call(
        relay_rows_kernel, [relay, relay], 0, 0, 4, [pltpu.SemaphoreType.DMA((2,))], True
    )(fwd, bwd, column_low, column_high)
    fwd, bwd = tie((fwd, bwd), (scan_token,))
    chunks += [fwd, bwd]

    fwd, bwd = shift(fwd, "tp", RING, 1), shift(bwd, "tp", RING, -1)
    relay_low, relay_high = shift(relay_low, "dp", 4, 1), shift(relay_high, "dp", 4, -1)
    half = ((TOKENS // 2, WIDTH), BF)
    last_low, last_high, weight = call(
        turn_kernel, [half, half, ((4, 4, 128, WIDTH), BF)], 7, 1 << 20, 1
    )(gated, fwd, bwd, column, column_low, column_high, relay_low, relay_high)
    chunks += [fwd, bwd]
    last_low, last_high = shift(last_low, "tp", RING, 1), shift(last_high, "tp", RING, -1)
    weight_other = swap_cores(weight)

    wide = ((3, WIDTH, WIDTH), BF)
    partial_sum, mine, other, block, weight_last = call(
        early_kernel, [(SQUARE, F32), wide, wide, (SQUARE, BF), (SQUARE, BF)], 10, 1 << 33
    )(*chunks, gated, weight, weight_other)
    ga, send, mine_last, other = call(
        late_kernel,
        [(SQUARE, BF), (STATE_GAIN, BF), (SQUARE, BF), ((4, WIDTH, WIDTH), BF)],
        10,
        1 << 31,
        0,
        [pltpu.VMEM(SQUARE, F32)],
    )(last_low, last_high, gated, block, weight_last, partial_sum, queries, att, gain_row, other)
    quarter, eighth = ((4, WIDTH, 128), BF), ((2 * WIDTH, 128), BF)
    part, up, down, low, high = call(
        combine_kernel,
        [quarter, quarter, quarter, eighth, eighth],
        3,
        1 << 20,
        0,
        [pltpu.VMEM(SQUARE, BF)],
    )(mine, swap_cores(other), mine_last)
    total, after = call(row_back_kernel, [(STATE_GAIN, BF), (STATE, F32)], 4, 1 << 22)(
        send, *[shift(send, "dp", 4, -k) for k in (1, 2, 3)]
    )
    up, down = call(relay_kernel, [quarter, quarter], 4, 1 << 20, 1)(
        total, up, down, shift(low, "dp", 4, 1), shift(high, "dp", 4, -1)
    )
    block = (WIDTH, 128)
    part, up, away, down = call(
        column_kernel,
        [(block, F32), (block, BF), (block, BF), (block, BF)],
        3,
        1 << 20,
        0,
        [pltpu.VMEM((4, WIDTH, 128), F32)],
    )(part, shift(up, "dp", 4, 1), shift(down, "dp", 4, -1))
    (weight_grad,) = call(sum_kernel, [((128, WIDTH), F32)], 4, 1 << 20)(
        part, shift(up, "y", 4, 1), shift(away, "y", 4, 2), shift(down, "y", 4, -1)
    )
    other = swap_cores(total)
    (both,) = call(pair_back_kernel, [(STATE_GAIN, BF)], 2, 1 << 22)(total, other)
    upper = [shift(both, "y", 4, -k) for k in (1, 2, 3)]
    query_grad, key_part, value_part = call(
        post_kernel, [(SQUARE, BF), (SQUARE, F32), (SQUARE, F32)], 5, 1 << 31
    )(queries, keys, values, ga, prior)
    key_grad, value_grad, gain_sum = call(
        final_kernel, [(SQUARE, BF), (SQUARE, BF), ((16, HEAD_DIM), F32)], 10, 1 << 28, 1
    )(down, keys, values, key_part, value_part, after, other, both, *upper)
    gain_grad = (gain_sum[0:4] + gain_sum[4:8]).reshape(WIDTH)
    return query_grad, key_grad, value_grad, gain_grad, weight_grad


def solution(mesh):
    grid = Mesh(mesh.devices.reshape(4, 2, RING, 4), ("y", "core", "tp", "dp"))
    rows = P(("y", "core", "dp"), "tp")
    return jax.shard_map(
        body,
        mesh=grid,
        in_specs=(rows, rows, rows, P("tp"), rows, rows),
        out_specs=(rows, rows, rows, P("tp"), rows),
        check_vma=False,
    )
```

```python
import math

import jax
import jax.numpy as jnp
from jax import lax
from jax.experimental import pallas as pl
from jax.experimental.pallas import tpu as pltpu
from jax.sharding import Mesh
from jax.sharding import PartitionSpec as P

HEAD_DIM = 128
HEADS = 4
TOKENS = 512
WIDTH = 512
RING = 8
EPS = 1e-06
SCALE = 1.0 / math.sqrt(16384.0)
BF = jnp.bfloat16
F32 = jnp.float32
PLANE = ("y", "dp")
BLOCKS = ("y", "core", "dp")
VMEM_LIMIT = 24 * 1024 * 1024
STATE = (HEADS * HEAD_DIM, HEAD_DIM)
STATE_GAIN = (HEADS * HEAD_DIM + 16, HEAD_DIM)
SQUARE = (TOKENS, WIDTH)
TOKEN = ((8, HEAD_DIM), jnp.float32)

NN = ((1,), (0,))
NT = ((1,), (1,))
TN = ((0,), (0,))


def dot(a, b, dims):
    return lax.dot_general(a, b, (dims, ((), ())), preferred_element_type=F32)


def span(h):
    return pl.ds(pl.multiple_of(h * HEAD_DIM, HEAD_DIM), HEAD_DIM)


def each(count, step):
    lax.fori_loop(0, count, lambda i, carry: (step(i), carry)[1], 0)


def causal_mask():
    rows = lax.broadcasted_iota(jnp.int32, (TOKENS, TOKENS), 0)
    cols = lax.broadcasted_iota(jnp.int32, (TOKENS, TOKENS), 1)
    return rows >= cols


def call(kernel, out, n_in, flops, any_in=0, scratch=(), any_out=False):
    vmem = pl.BlockSpec(memory_space=pltpu.VMEM)
    anys = pl.BlockSpec(memory_space=pl.ANY)
    return pl.pallas_call(
        kernel,
        out_shape=tuple(jax.ShapeDtypeStruct(s, d) for s, d in out),
        in_specs=[anys] * any_in + [vmem] * n_in,
        out_specs=tuple(anys if any_out else vmem for _ in out),
        scratch_shapes=scratch,
        compiler_params=pltpu.CompilerParams(vmem_limit_bytes=VMEM_LIMIT),
        cost_estimate=pl.CostEstimate(flops=flops, bytes_accessed=4 << 20, transcendentals=0),
    )


def state_kernel(k_ref, v_ref, out_ref, token_ref):
    token_ref[...] = jnp.zeros(TOKEN[0], F32)

    def step(h):
        state = dot(k_ref[:, span(h)], v_ref[:, span(h)], TN).astype(BF)
        out_ref[pl.ds(h * 8, 8)] = state.reshape(8, 16, HEAD_DIM)

    each(HEADS, step)


def scan_kernel(in_ref, out_ref, token_ref):
    token_ref[...] = jnp.zeros(TOKEN[0], F32)
    total = jnp.zeros((16, HEAD_DIM), F32)
    for c in range(32):
        out_ref[c] = total.astype(BF)
        total = total + in_ref[c].astype(F32)


def when(flag):
    return jnp.where(flag, 1.0, 0.0).astype(F32)


def norm_kernel(q_ref, k_ref, v_ref, gain_ref, prior_ref, att_ref, gated_ref):
    mask = causal_mask()

    def step(h):
        cols = span(h)
        scores = dot(q_ref[:, cols], k_ref[:, cols], NT)
        scores = jnp.where(mask, scores, 0.0).astype(BF)
        att = dot(scores, v_ref[:, cols], NN) + dot(q_ref[:, cols], prior_ref[cols], NN)
        att_ref[:, cols] = att
        inverse = lax.rsqrt(jnp.mean(att * att, axis=-1, keepdims=True) + EPS)
        gated = (att * inverse * gain_ref[:, cols]).astype(BF)
        gated_ref[cols, :] = gated.T

    each(HEADS, step)


def is_same():
    return lax.rem(lax.axis_index("tp"), 2) == lax.axis_index("core")


def row_of(k):
    return lax.div(lax.rem(lax.axis_index("tp") + k + RING, RING), 2)


EVENS = (0, 2, -2, 4)
ODDS = (1, -1, 3, -3)


ORDER = (0, 2, -2, 1, -1, 3, -3)


def early_kernel(*refs):
    own, f1, b1, f2, b2, f3, b3, gated_ref, wm_ref, wo_ref = refs[:10]
    sum_ref, part_ref, weight_ref, rows, sems = refs[10:]
    copies = []
    for n, ref in enumerate((own, b2, f2, b1, f1, b3, f3)):
        copies.append(pltpu.make_async_copy(ref, rows.at[n], sems.at[n]))
    for c in copies:
        c.start()
    for c in copies:
        c.wait()
    sum_ref[...] = jnp.zeros(SQUARE, F32)
    same = is_same()

    def offset(n):
        k = jnp.int32(ORDER[-1])
        for i in range(len(ORDER) - 1):
            k = jnp.where(n == i, ORDER[i], k)
        return k

    def fetch(even, k):
        mine = jnp.logical_not(jnp.logical_xor(same, even))
        y = row_of(k)

        @pl.when(mine)
        def _():
            weight_ref[...] = wm_ref[y].reshape(SQUARE)

        @pl.when(jnp.logical_not(mine))
        def _():
            weight_ref[...] = wo_ref[y].reshape(SQUARE)

    def step(n):
        slot = jnp.where(n < 3, n, n + 1)
        part_ref[slot] = dot(gated_ref[...], rows[n], NN).astype(BF)
        fetch(n < 3, offset(n))
        sum_ref[...] += dot(rows[n], weight_ref[...], NN)

    each(7, step)
    fetch(jnp.bool_(True), jnp.int32(4))


def last_kernel(low_ref, high_ref, gated_ref, part_ref, last_ref, other_ref):
    half = TOKENS // 2
    last = dot(gated_ref[:, 0:half], low_ref[...], NN)
    last_ref[...] = (last + dot(gated_ref[:, half:TOKENS], high_ref[...], NN)).astype(BF)
    base = jnp.where(is_same(), 4, 0)

    def step(s):
        other_ref[s] = part_ref[base + s]

    each(3, step)

    @pl.when(is_same())
    def _():
        other_ref[3] = part_ref[7]

    @pl.when(jnp.logical_not(is_same()))
    def _():
        other_ref[3] = last_ref[...]


def grad_kernel(
    low_ref, high_ref, weight_ref, sum_ref, q_ref, att_ref, gain_ref, ga_ref, send_ref, acc
):
    half = TOKENS // 2
    acc[0:half] = sum_ref[0:half] + dot(low_ref[...], weight_ref[...], NN)
    acc[half:TOKENS] = sum_ref[half:TOKENS] + dot(high_ref[...], weight_ref[...], NN)
    grad_rows(acc, q_ref, att_ref, gain_ref, ga_ref, send_ref)


def combine_kernel(
    part_ref, got_ref, last_ref, own_ref, up_ref, down_ref, low_ref, high_ref, rows
):
    place = lax.axis_index("dp")
    same = is_same()
    base = jnp.where(same, 0, 4)

    def step(s):
        late = jnp.logical_and(same, s == 3)

        @pl.when(late)
        def _():
            rows[...] = (last_ref[...].astype(F32) + got_ref[s].astype(F32)).astype(BF)

        @pl.when(jnp.logical_not(late))
        def _():
            rows[...] = (part_ref[base + s].astype(F32) + got_ref[s].astype(F32)).astype(BF)

        blocks = []
        for d in range(4):
            start = pl.multiple_of(lax.rem(place + d, 4) * 128, 128)
            blocks.append(rows[:, pl.ds(start, 128)])
        own_ref[s], up_ref[s], down_ref[s] = blocks[0], blocks[1], blocks[3]
        at = pl.ds(pl.multiple_of(s * 256, 256), 256)
        low_ref[at], high_ref[at] = blocks[2][0:256], blocks[2][256:512]

    each(4, step)


def pack_kernel(after1_ref, after2_ref, own_ref, r1_ref, r2_ref, r3_ref, out_ref, token_ref):
    token_ref[...] = jnp.zeros(TOKEN[0], F32)
    y = lax.axis_index("y")
    for k, ref in enumerate((own_ref, r1_ref, r2_ref, r3_ref)):
        out_ref[lax.rem(y + 4 - k, 4)] = ref[...]


def relay_rows_kernel(after1_ref, after2_ref, low_ref, high_ref, low_out, high_out, sems):
    low = pltpu.make_async_copy(low_ref.at[0:2], low_out, sems.at[0])
    high = pltpu.make_async_copy(high_ref.at[2:4], high_out, sems.at[1])
    low.start()
    high.start()
    low.wait()
    high.wait()


def turn_kernel(
    after_ref, fwd_ref, bwd_ref, own_ref, low_ref, high_ref, far_low_ref, far_high_ref,
    fwd_out, bwd_out, out_ref,
):
    fwd_out[...] = fwd_ref[0 : TOKENS // 2]
    bwd_out[...] = bwd_ref[TOKENS // 2 : TOKENS]
    x = lax.axis_index("dp")
    for k, ref in ((0, own_ref), (3, low_ref), (1, high_ref)):
        for y in range(4):
            out_ref[y, lax.rem(x + k, 4)] = ref[y]
    for y in range(2):
        out_ref[y, lax.rem(x + 2, 4)] = far_low_ref[y]
        out_ref[2 + y, lax.rem(x + 2, 4)] = far_high_ref[y]


def tie(values, deps):
    def kernel(*refs):
        pass

    n = len(values)
    anys = pl.BlockSpec(memory_space=pl.ANY)
    vmem = pl.BlockSpec(memory_space=pltpu.VMEM)
    return pl.pallas_call(
        kernel,
        out_shape=tuple(jax.ShapeDtypeStruct(v.shape, v.dtype) for v in values),
        in_specs=[anys] * n + [vmem] * len(deps),
        out_specs=(anys,) * n,
        input_output_aliases={i: i for i in range(n)},
        cost_estimate=pl.CostEstimate(flops=0, bytes_accessed=0, transcendentals=0),
    )(*values, *deps)


def relay_kernel(after_ref, up_ref, down_ref, low_ref, high_ref, up_out, down_out):
    def step(y):
        rows = pl.ds(pl.multiple_of(y * 256, 256), 256)
        up_out[y, 0:256] = (up_ref[y, 0:256].astype(F32) + low_ref[rows].astype(F32)).astype(BF)
        up_out[y, 256:512] = up_ref[y, 256:512]
        down_out[y, 0:256] = down_ref[y, 0:256]
        low = down_ref[y, 256:512].astype(F32) + high_ref[rows].astype(F32)
        down_out[y, 256:512] = low.astype(BF)

    each(4, step)


def column_kernel(after_ref, own_ref, a_ref, b_ref, own_out, up_out, far_out, down_out, rows):
    same = is_same()

    def step(s):
        k = jnp.where(s == 3, 4, jnp.where(s == 2, -2, s * 2))
        odd = jnp.where(s == 3, -3, jnp.where(s == 2, 3, 1 - 2 * s))
        y = row_of(jnp.where(same, k, odd))
        total = own_ref[s].astype(F32) + a_ref[s].astype(F32) + b_ref[s].astype(F32)
        rows[lax.rem(y + 4 - lax.axis_index("y"), 4)] = total

    each(4, step)
    own_out[...] = rows[0]
    up_out[...] = rows[1].astype(BF)
    far_out[...] = rows[2].astype(BF)
    down_out[...] = rows[3].astype(BF)


def grad_rows(own_ref, q_ref, att_ref, gain_ref, ga_ref, send_ref):
    base = HEADS * HEAD_DIM
    rows = lax.broadcasted_iota(jnp.int32, (16, HEAD_DIM), 0)

    def step(h, sums):
        att = att_ref[:, span(h)]
        inverse = lax.rsqrt(jnp.mean(att * att, axis=-1, keepdims=True) + EPS)
        normed = att * inverse
        grad = own_ref[:, span(h)]
        part = jnp.sum(grad * normed, axis=0, keepdims=True)
        high = part.astype(BF).astype(F32)
        sums = sums + jnp.where(rows == h, high, 0.0) + jnp.where(rows == 4 + h, part - high, 0.0)
        grad = grad * gain_ref[:, span(h)]
        grad = (grad - normed * jnp.mean(grad * normed, axis=-1, keepdims=True)) * inverse
        grad = grad.astype(BF)
        ga_ref[:, span(h)] = grad
        send_ref[span(h)] = dot(q_ref[:, span(h)], grad, TN).astype(BF)
        return sums

    sums = lax.fori_loop(0, HEADS, step, jnp.zeros((16, HEAD_DIM), F32))
    send_ref[base:] = sums.astype(BF)


def resum(parts):
    total = sum(p.astype(F32) for p in parts)
    gain = total[0:4] + total[4:8]
    high = gain.astype(BF).astype(F32)
    return jnp.concatenate([high, gain - high, jnp.zeros((8, HEAD_DIM), F32)], axis=0)


def row_back_kernel(own_ref, r1_ref, r2_ref, r3_ref, total_ref, after_ref):
    x = lax.axis_index("dp")
    base = HEADS * HEAD_DIM
    r1, r2, r3 = (r[0:base].astype(F32) for r in (r1_ref, r2_ref, r3_ref))
    after_ref[...] = r1 * when(x <= 2) + r2 * when(x <= 1) + r3 * when(x <= 0)
    total_ref[0:base] = (own_ref[0:base].astype(F32) + r1 + r2 + r3).astype(BF)
    total_ref[base:] = resum([r[base:] for r in (own_ref, r1_ref, r2_ref, r3_ref)]).astype(BF)


def pair_back_kernel(total_ref, other_ref, out_ref):
    base = HEADS * HEAD_DIM
    out_ref[0:base] = (total_ref[0:base].astype(F32) + other_ref[0:base].astype(F32)).astype(BF)
    out_ref[base:] = resum([total_ref[base:], other_ref[base:]]).astype(BF)


def post_kernel(q_ref, k_ref, v_ref, ga_ref, prior_ref, qg_ref, kp_ref, vp_ref, token_ref):
    token_ref[...] = jnp.zeros(TOKEN[0], F32)
    mask = causal_mask()

    def step(h):
        cols = span(h)
        q, k, v, ga = q_ref[:, cols], k_ref[:, cols], v_ref[:, cols], ga_ref[:, cols]
        scores = jnp.where(mask, dot(q, k, NT), 0.0).astype(BF)
        vp_ref[:, cols] = dot(scores, ga, TN)
        back = jnp.where(mask, dot(ga, v, NT), 0.0).astype(BF)
        qg_ref[:, cols] = (dot(back, k, NN) + dot(ga, prior_ref[cols], NT)).astype(BF)
        kp_ref[:, cols] = dot(back, q, TN)

    each(HEADS, step)


def final_kernel(
    after_last_ref, k_ref, v_ref, kp_ref, vp_ref, after_ref, other_ref, own, u1, u2, u3, kg_ref, vg_ref, gain_ref
):
    base = HEADS * HEAD_DIM
    y = lax.axis_index("y")
    first = when(lax.axis_index("core") == 0)

    def step(h):
        cols = span(h)
        later = after_ref[cols] + other_ref[cols].astype(F32) * first
        later = later + u1[cols].astype(F32) * when(y <= 2) + u2[cols].astype(F32) * when(y <= 1)
        later = (later + u3[cols].astype(F32) * when(y <= 0)).astype(BF)
        kg_ref[:, cols] = (kp_ref[:, cols] + dot(v_ref[:, cols], later, NT)).astype(BF)
        vg_ref[:, cols] = (vp_ref[:, cols] + dot(k_ref[:, cols], later, NN)).astype(BF)

    each(HEADS, step)
    gain = resum([r[base:] for r in (own, u1, u2, u3)])
    gain_ref[...] = (gain[0:4] + gain[4:8]) * SCALE


def sum_kernel(own_ref, r1_ref, r2_ref, r3_ref, out_ref):
    total = own_ref[...]
    for ref in (r1_ref, r2_ref, r3_ref):
        total = total + ref[...].astype(F32)
    out_ref[...] = (total * SCALE).T


def shift(x, axis, size, k, wrap=True):
    pairs = [(i, (i + k) % size) for i in range(size) if wrap or 0 <= i + k < size]
    return lax.ppermute(x, axis, pairs)


def swap_cores(x):
    return lax.ppermute(x, "core", [(0, 1), (1, 0)])


def body(queries, keys, values, gain, out_weight, out_cotangent):
    own = out_cotangent
    fwd, bwd = shift(own, "tp", RING, 1), shift(own, "tp", RING, -1)
    slices = ((32, 16, HEAD_DIM), BF)
    state, state_token = call(state_kernel, [slices, TOKEN], 2, 1 << 27)(keys, values)
    states = lax.all_to_all(state, BLOCKS, 0, 0, tiled=True)
    others = [shift(out_weight, "y", 4, k) for k in (1, 2, 3)]
    column, column_token = call(pack_kernel, [((4, 128, WIDTH), BF), TOKEN], 4, 1 << 20, 2)(
        fwd, bwd, out_weight, *others
    )
    fwd, bwd = tie((fwd, bwd), (state_token, column_token))
    chunks = [own, fwd, bwd]

    fwd, bwd = shift(fwd, "tp", RING, 1), shift(bwd, "tp", RING, -1)
    priors, scan_token = call(scan_kernel, [slices, TOKEN], 1, 1 << 20)(states)
    prior = lax.all_to_all(priors, BLOCKS, 0, 0, tiled=True).reshape(STATE)
    column_low, column_high = shift(column, "dp", 4, 1), shift(column, "dp", 4, -1)
    gain_row = gain.reshape(1, WIDTH)
    att, gated = call(norm_kernel, [(SQUARE, F32), (SQUARE, BF)], 5, 1 << 30)(
        queries, keys, values, gain_row, prior
    )
    relay = ((2, 128, WIDTH), BF)
    relay_low, relay_high = call(
        relay_rows_kernel, [relay, relay], 0, 0, 4, [pltpu.SemaphoreType.DMA((2,))], True
    )(fwd, bwd, column_low, column_high)
    fwd, bwd = tie((fwd, bwd), (scan_token,))
    chunks += [fwd, bwd]

    fwd, bwd = shift(fwd, "tp", RING, 1), shift(bwd, "tp", RING, -1)
    relay_low, relay_high = shift(relay_low, "dp", 4, 1), shift(relay_high, "dp", 4, -1)
    half = ((TOKENS // 2, WIDTH), BF)
    last_low, last_high, weight = call(
        turn_kernel, [half, half, ((4, 4, 128, WIDTH), BF)], 7, 1 << 20, 1
    )(gated, fwd, bwd, column, column_low, column_high, relay_low, relay_high)
    chunks += [fwd, bwd]
    last_low, last_high = shift(last_low, "tp", RING, 1), shift(last_high, "tp", RING, -1)
    weight_other = swap_cores(weight)

    wide = ((8, WIDTH, WIDTH), BF)
    partial_sum, parts, weight_last = call(
        early_kernel,
        [(SQUARE, F32), wide, (SQUARE, BF)],
        3,
        1 << 33,
        7,
        [pltpu.VMEM((7, TOKENS, WIDTH), BF), pltpu.SemaphoreType.DMA((7,))],
    )(*chunks, gated, weight, weight_other)
    last, other = call(last_kernel, [(SQUARE, BF), ((4, WIDTH, WIDTH), BF)], 4, 1 << 29)(
        last_low, last_high, gated, parts
    )
    ga, send = call(
        grad_kernel,
        [(SQUARE, BF), (STATE_GAIN, BF)],
        7,
        1 << 30,
        0,
        [pltpu.VMEM(SQUARE, F32)],
    )(last_low, last_high, weight_last, partial_sum, queries, att, gain_row)
    quarter, eighth = ((4, WIDTH, 128), BF), ((2 * WIDTH, 128), BF)
    part, up, down, low, high = call(
        combine_kernel,
        [quarter, quarter, quarter, eighth, eighth],
        3,
        1 << 20,
        0,
        [pltpu.VMEM(SQUARE, BF)],
    )(parts, swap_cores(other), last)
    total, after = call(row_back_kernel, [(STATE_GAIN, BF), (STATE, F32)], 4, 1 << 22)(
        send, *[shift(send, "dp", 4, -k) for k in (1, 2, 3)]
    )
    up, down = call(relay_kernel, [quarter, quarter], 4, 1 << 20, 1)(
        total, up, down, shift(low, "dp", 4, 1), shift(high, "dp", 4, -1)
    )
    query_grad, key_part, value_part, token = call(
        post_kernel, [(SQUARE, BF), (SQUARE, F32), (SQUARE, F32), TOKEN], 5, 1 << 31
    )(queries, keys, values, ga, prior)
    block = (WIDTH, 128)
    part, up, away, down = call(
        column_kernel,
        [(block, F32), (block, BF), (block, BF), (block, BF)],
        4,
        1 << 20,
        0,
        [pltpu.VMEM((4, WIDTH, 128), F32)],
    )(token, part, shift(up, "dp", 4, 1), shift(down, "dp", 4, -1))
    (weight_grad,) = call(sum_kernel, [((128, WIDTH), F32)], 4, 1 << 20)(
        part, shift(up, "y", 4, 1), shift(away, "y", 4, 2), shift(down, "y", 4, -1)
    )
    other = swap_cores(total)
    (both,) = call(pair_back_kernel, [(STATE_GAIN, BF)], 2, 1 << 22)(total, other)
    upper = [shift(both, "y", 4, -k) for k in (1, 2, 3)]
    key_grad, value_grad, gain_sum = call(
        final_kernel, [(SQUARE, BF), (SQUARE, BF), ((HEADS, HEAD_DIM), F32)], 10, 1 << 28, 1
    )(down, keys, values, key_part, value_part, after, other, both, *upper)
    gain_grad = gain_sum.reshape(WIDTH)
    return query_grad, key_grad, value_grad, gain_grad, weight_grad


def solution(mesh):
    grid = Mesh(mesh.devices.reshape(4, 2, RING, 4), ("y", "core", "tp", "dp"))
    rows = P(("y", "core", "dp"), "tp")
    return jax.shard_map(
        body,
        mesh=grid,
        in_specs=(rows, rows, rows, P("tp"), rows, rows),
        out_specs=(rows, rows, rows, P("tp"), rows),
        check_vma=False,
    )
```

```python
import math

import jax
import jax.numpy as jnp
from jax import lax
from jax.experimental import pallas as pl
from jax.experimental.pallas import tpu as pltpu
from jax.sharding import Mesh
from jax.sharding import PartitionSpec as P

HEAD_DIM = 128
HEADS = 4
TOKENS = 512
WIDTH = 512
RING = 8
EPS = 1e-06
SCALE = 1.0 / math.sqrt(16384.0)
BF = jnp.bfloat16
F32 = jnp.float32
PLANE = ("y", "dp")
BLOCKS = ("y", "core", "dp")
VMEM_LIMIT = 24 * 1024 * 1024
STATE = (HEADS * HEAD_DIM, HEAD_DIM)
STATE_GAIN = (HEADS * HEAD_DIM + 16, HEAD_DIM)
SQUARE = (TOKENS, WIDTH)
TOKEN = ((8, HEAD_DIM), jnp.float32)

NN = ((1,), (0,))
NT = ((1,), (1,))
TN = ((0,), (0,))


def dot(a, b, dims):
    return lax.dot_general(a, b, (dims, ((), ())), preferred_element_type=F32)


def span(h):
    return pl.ds(pl.multiple_of(h * HEAD_DIM, HEAD_DIM), HEAD_DIM)


def each(count, step, unroll=1):
    lax.fori_loop(0, count, lambda i, carry: (step(i), carry)[1], 0, unroll=unroll)


def causal_mask():
    rows = lax.broadcasted_iota(jnp.int32, (TOKENS, TOKENS), 0)
    cols = lax.broadcasted_iota(jnp.int32, (TOKENS, TOKENS), 1)
    return rows >= cols


def call(kernel, out, n_in, flops, any_in=0, scratch=(), any_out=False):
    vmem = pl.BlockSpec(memory_space=pltpu.VMEM)
    anys = pl.BlockSpec(memory_space=pl.ANY)
    return pl.pallas_call(
        kernel,
        out_shape=tuple(jax.ShapeDtypeStruct(s, d) for s, d in out),
        in_specs=[anys] * any_in + [vmem] * n_in,
        out_specs=tuple(anys if any_out else vmem for _ in out),
        scratch_shapes=scratch,
        compiler_params=pltpu.CompilerParams(vmem_limit_bytes=VMEM_LIMIT),
        cost_estimate=pl.CostEstimate(flops=flops, bytes_accessed=4 << 20, transcendentals=0),
    )


def state_kernel(k_ref, v_ref, out_ref, token_ref):
    token_ref[...] = jnp.zeros(TOKEN[0], F32)

    def step(h):
        state = dot(k_ref[:, span(h)], v_ref[:, span(h)], TN).astype(BF)
        out_ref[pl.ds(h * 8, 8)] = state.reshape(8, 16, HEAD_DIM)

    each(HEADS, step)


def scan_kernel(in_ref, out_ref, token_ref):
    token_ref[...] = jnp.zeros(TOKEN[0], F32)
    total = jnp.zeros((16, HEAD_DIM), F32)
    for c in range(32):
        out_ref[c] = total.astype(BF)
        total = total + in_ref[c].astype(F32)


def when(flag):
    return jnp.where(flag, 1.0, 0.0).astype(F32)


def norm_kernel(q_ref, k_ref, v_ref, gain_ref, prior_ref, att_ref, gated_ref):
    mask = causal_mask()

    def step(h):
        cols = span(h)
        scores = dot(q_ref[:, cols], k_ref[:, cols], NT)
        scores = jnp.where(mask, scores, 0.0).astype(BF)
        att = dot(scores, v_ref[:, cols], NN) + dot(q_ref[:, cols], prior_ref[cols], NN)
        att_ref[:, cols] = att
        inverse = lax.rsqrt(jnp.mean(att * att, axis=-1, keepdims=True) + EPS)
        gated = (att * inverse * gain_ref[:, cols]).astype(BF)
        gated_ref[cols, :] = gated.T

    each(HEADS, step, 2)


def is_same():
    return lax.rem(lax.axis_index("tp"), 2) == lax.axis_index("core")


def row_of(k):
    return lax.div(lax.rem(lax.axis_index("tp") + k + RING, RING), 2)


EVENS = (0, 2, -2, 4)
ODDS = (1, -1, 3, -3)


ORDER = (0, 2, -2, 1, -1, 3, -3)


def early_kernel(*refs):
    own, f1, b1, f2, b2, f3, b3, gated_ref, wm_ref, wo_ref = refs[:10]
    sum_ref, part_ref, weight_ref, rows, sems = refs[10:]
    copies = []
    for n, ref in enumerate((own, b2, f2, b1, f1, b3, f3)):
        copies.append(pltpu.make_async_copy(ref, rows.at[n], sems.at[n]))
    for c in copies:
        c.start()
    for c in copies:
        c.wait()
    sum_ref[...] = jnp.zeros(SQUARE, F32)
    same = is_same()

    def offset(n):
        k = jnp.int32(ORDER[-1])
        for i in range(len(ORDER) - 1):
            k = jnp.where(n == i, ORDER[i], k)
        return k

    def fetch(even, k, slot):
        mine = jnp.logical_not(jnp.logical_xor(same, even))
        y = row_of(k)

        @pl.when(mine)
        def _():
            weight_ref[slot] = wm_ref[y].reshape(SQUARE)

        @pl.when(jnp.logical_not(mine))
        def _():
            weight_ref[slot] = wo_ref[y].reshape(SQUARE)

    def part(n):
        part_ref[jnp.where(n < 3, n, n + 1)] = dot(gated_ref[...], rows[n], NN).astype(BF)

    def step(i):
        n = 2 * i
        for m in range(2):
            fetch(n + m < 3, offset(n + m), m)
            part(n + m)
        first = dot(rows[n], weight_ref[0], NN)
        sum_ref[...] += first + dot(rows[n + 1], weight_ref[1], NN)

    each(3, step)
    fetch(jnp.bool_(False), jnp.int32(ORDER[6]), 0)
    part(jnp.int32(6))
    sum_ref[...] += dot(rows[6], weight_ref[0], NN)
    fetch(jnp.bool_(True), jnp.int32(4), 0)


def last_kernel(low_ref, high_ref, gated_ref, part_ref, last_ref, other_ref):
    half = TOKENS // 2
    last = dot(gated_ref[:, 0:half], low_ref[...], NN)
    last_ref[...] = (last + dot(gated_ref[:, half:TOKENS], high_ref[...], NN)).astype(BF)
    base = jnp.where(is_same(), 4, 0)

    def step(s):
        other_ref[s] = part_ref[base + s]

    each(3, step)

    @pl.when(is_same())
    def _():
        other_ref[3] = part_ref[7]

    @pl.when(jnp.logical_not(is_same()))
    def _():
        other_ref[3] = last_ref[...]


def grad_kernel(
    low_ref, high_ref, weight_ref, sum_ref, q_ref, att_ref, gain_ref, ga_ref, send_ref, token_ref, acc
):
    token_ref[...] = jnp.zeros(TOKEN[0], F32)
    half = TOKENS // 2
    acc[0:half] = sum_ref[0:half] + dot(low_ref[...], weight_ref[0], NN)
    acc[half:TOKENS] = sum_ref[half:TOKENS] + dot(high_ref[...], weight_ref[0], NN)
    grad_rows(acc, q_ref, att_ref, gain_ref, ga_ref, send_ref)


def combine_kernel(
    after_ref, part_ref, got_ref, last_ref, own_ref, up_ref, down_ref, low_ref, high_ref, rows
):
    place = lax.axis_index("dp")
    same = is_same()
    base = jnp.where(same, 0, 4)

    def step(s):
        late = jnp.logical_and(same, s == 3)

        @pl.when(late)
        def _():
            rows[...] = (last_ref[...].astype(F32) + got_ref[s].astype(F32)).astype(BF)

        @pl.when(jnp.logical_not(late))
        def _():
            rows[...] = (part_ref[base + s].astype(F32) + got_ref[s].astype(F32)).astype(BF)

        blocks = []
        for d in range(4):
            start = pl.multiple_of(lax.rem(place + d, 4) * 128, 128)
            blocks.append(rows[:, pl.ds(start, 128)])
        own_ref[s], up_ref[s], down_ref[s] = blocks[0], blocks[1], blocks[3]
        at = pl.ds(pl.multiple_of(s * 256, 256), 256)
        low_ref[at], high_ref[at] = blocks[2][0:256], blocks[2][256:512]

    each(4, step)


def pack_kernel(after1_ref, after2_ref, own_ref, r1_ref, r2_ref, r3_ref, out_ref, token_ref):
    token_ref[...] = jnp.zeros(TOKEN[0], F32)
    y = lax.axis_index("y")
    for k, ref in enumerate((own_ref, r1_ref, r2_ref, r3_ref)):
        out_ref[lax.rem(y + 4 - k, 4)] = ref[...]


def relay_rows_kernel(after1_ref, after2_ref, low_ref, high_ref, low_out, high_out, sems):
    low = pltpu.make_async_copy(low_ref.at[0:2], low_out, sems.at[0])
    high = pltpu.make_async_copy(high_ref.at[2:4], high_out, sems.at[1])
    low.start()
    high.start()
    low.wait()
    high.wait()


def turn_kernel(
    after_ref, fwd_ref, bwd_ref, own_ref, low_ref, high_ref, far_low_ref, far_high_ref,
    fwd_out, bwd_out, out_ref,
):
    fwd_out[...] = fwd_ref[0 : TOKENS // 2]
    bwd_out[...] = bwd_ref[TOKENS // 2 : TOKENS]
    x = lax.axis_index("dp")
    for k, ref in ((0, own_ref), (3, low_ref), (1, high_ref)):
        for y in range(4):
            out_ref[y, lax.rem(x + k, 4)] = ref[y]
    for y in range(2):
        out_ref[y, lax.rem(x + 2, 4)] = far_low_ref[y]
        out_ref[2 + y, lax.rem(x + 2, 4)] = far_high_ref[y]


def tie(values, deps):
    def kernel(*refs):
        pass

    n = len(values)
    anys = pl.BlockSpec(memory_space=pl.ANY)
    vmem = pl.BlockSpec(memory_space=pltpu.VMEM)
    return pl.pallas_call(
        kernel,
        out_shape=tuple(jax.ShapeDtypeStruct(v.shape, v.dtype) for v in values),
        in_specs=[anys] * n + [vmem] * len(deps),
        out_specs=(anys,) * n,
        input_output_aliases={i: i for i in range(n)},
        cost_estimate=pl.CostEstimate(flops=0, bytes_accessed=0, transcendentals=0),
    )(*values, *deps)


def relay_kernel(after_ref, up_ref, down_ref, low_ref, high_ref, up_out, down_out):
    def step(y):
        rows = pl.ds(pl.multiple_of(y * 256, 256), 256)
        up_out[y, 0:256] = (up_ref[y, 0:256].astype(F32) + low_ref[rows].astype(F32)).astype(BF)
        up_out[y, 256:512] = up_ref[y, 256:512]
        down_out[y, 0:256] = down_ref[y, 0:256]
        low = down_ref[y, 256:512].astype(F32) + high_ref[rows].astype(F32)
        down_out[y, 256:512] = low.astype(BF)

    each(4, step)


def column_kernel(after_ref, own_ref, a_ref, b_ref, own_out, up_out, far_out, down_out, rows):
    same = is_same()

    def step(s):
        k = jnp.where(s == 3, 4, jnp.where(s == 2, -2, s * 2))
        odd = jnp.where(s == 3, -3, jnp.where(s == 2, 3, 1 - 2 * s))
        y = row_of(jnp.where(same, k, odd))
        total = own_ref[s].astype(F32) + a_ref[s].astype(F32) + b_ref[s].astype(F32)
        rows[lax.rem(y + 4 - lax.axis_index("y"), 4)] = total

    each(4, step)
    own_out[...] = rows[0]
    up_out[...] = rows[1].astype(BF)
    far_out[...] = rows[2].astype(BF)
    down_out[...] = rows[3].astype(BF)


def grad_rows(own_ref, q_ref, att_ref, gain_ref, ga_ref, send_ref):
    base = HEADS * HEAD_DIM
    rows = lax.broadcasted_iota(jnp.int32, (16, HEAD_DIM), 0)

    def step(h, sums):
        att = att_ref[:, span(h)]
        inverse = lax.rsqrt(jnp.mean(att * att, axis=-1, keepdims=True) + EPS)
        normed = att * inverse
        grad = own_ref[:, span(h)]
        part = jnp.sum(grad * normed, axis=0, keepdims=True)
        high = part.astype(BF).astype(F32)
        sums = sums + jnp.where(rows == h, high, 0.0) + jnp.where(rows == 4 + h, part - high, 0.0)
        grad = grad * gain_ref[:, span(h)]
        grad = (grad - normed * jnp.mean(grad * normed, axis=-1, keepdims=True)) * inverse
        grad = grad.astype(BF)
        ga_ref[:, span(h)] = grad
        send_ref[span(h)] = dot(q_ref[:, span(h)], grad, TN).astype(BF)
        return sums

    sums = lax.fori_loop(0, HEADS, step, jnp.zeros((16, HEAD_DIM), F32), unroll=2)
    send_ref[base:] = sums.astype(BF)


def resum(parts):
    total = sum(p.astype(F32) for p in parts)
    gain = total[0:4] + total[4:8]
    high = gain.astype(BF).astype(F32)
    return jnp.concatenate([high, gain - high, jnp.zeros((8, HEAD_DIM), F32)], axis=0)


def row_back_kernel(own_ref, r1_ref, r2_ref, r3_ref, total_ref, after_ref):
    x = lax.axis_index("dp")
    base = HEADS * HEAD_DIM
    r1, r2, r3 = (r[0:base].astype(F32) for r in (r1_ref, r2_ref, r3_ref))
    after_ref[...] = r1 * when(x <= 2) + r2 * when(x <= 1) + r3 * when(x <= 0)
    total_ref[0:base] = (own_ref[0:base].astype(F32) + r1 + r2 + r3).astype(BF)
    total_ref[base:] = resum([r[base:] for r in (own_ref, r1_ref, r2_ref, r3_ref)]).astype(BF)


def pair_back_kernel(total_ref, other_ref, out_ref):
    base = HEADS * HEAD_DIM
    out_ref[0:base] = (total_ref[0:base].astype(F32) + other_ref[0:base].astype(F32)).astype(BF)
    out_ref[base:] = resum([total_ref[base:], other_ref[base:]]).astype(BF)


def post_kernel(q_ref, k_ref, v_ref, ga_ref, prior_ref, qg_ref, kp_ref, vp_ref, token_ref):
    token_ref[...] = jnp.zeros(TOKEN[0], F32)
    mask = causal_mask()

    def step(h):
        cols = span(h)
        q, k, v, ga = q_ref[:, cols], k_ref[:, cols], v_ref[:, cols], ga_ref[:, cols]
        scores = jnp.where(mask, dot(q, k, NT), 0.0).astype(BF)
        vp_ref[:, cols] = dot(scores, ga, TN)
        back = jnp.where(mask, dot(ga, v, NT), 0.0).astype(BF)
        qg_ref[:, cols] = (dot(back, k, NN) + dot(ga, prior_ref[cols], NT)).astype(BF)
        kp_ref[:, cols] = dot(back, q, TN)

    each(HEADS, step)


def final_kernel(
    after_last_ref, k_ref, v_ref, kp_ref, vp_ref, after_ref, other_ref, own, u1, u2, u3, kg_ref, vg_ref, gain_ref
):
    base = HEADS * HEAD_DIM
    y = lax.axis_index("y")
    first = when(lax.axis_index("core") == 0)

    def step(h):
        cols = span(h)
        later = after_ref[cols] + other_ref[cols].astype(F32) * first
        later = later + u1[cols].astype(F32) * when(y <= 2) + u2[cols].astype(F32) * when(y <= 1)
        later = (later + u3[cols].astype(F32) * when(y <= 0)).astype(BF)
        kg_ref[:, cols] = (kp_ref[:, cols] + dot(v_ref[:, cols], later, NT)).astype(BF)
        vg_ref[:, cols] = (vp_ref[:, cols] + dot(k_ref[:, cols], later, NN)).astype(BF)

    each(HEADS, step, 2)
    gain = resum([r[base:] for r in (own, u1, u2, u3)])
    gain_ref[...] = (gain[0:4] + gain[4:8]) * SCALE


def sum_kernel(own_ref, r1_ref, r2_ref, r3_ref, out_ref):
    total = own_ref[...]
    for ref in (r1_ref, r2_ref, r3_ref):
        total = total + ref[...].astype(F32)
    out_ref[...] = (total * SCALE).T


def shift(x, axis, size, k, wrap=True):
    pairs = [(i, (i + k) % size) for i in range(size) if wrap or 0 <= i + k < size]
    return lax.ppermute(x, axis, pairs)


def swap_cores(x):
    return lax.ppermute(x, "core", [(0, 1), (1, 0)])


def body(queries, keys, values, gain, out_weight, out_cotangent):
    own = out_cotangent
    fwd, bwd = shift(own, "tp", RING, 1), shift(own, "tp", RING, -1)
    slices = ((32, 16, HEAD_DIM), BF)
    state, state_token = call(state_kernel, [slices, TOKEN], 2, 1 << 27)(keys, values)
    states = lax.all_to_all(state, BLOCKS, 0, 0, tiled=True)
    others = [shift(out_weight, "y", 4, k) for k in (1, 2, 3)]
    column, column_token = call(pack_kernel, [((4, 128, WIDTH), BF), TOKEN], 4, 1 << 20, 2)(
        fwd, bwd, out_weight, *others
    )
    fwd, bwd = tie((fwd, bwd), (state_token, column_token))
    chunks = [own, fwd, bwd]

    fwd, bwd = shift(fwd, "tp", RING, 1), shift(bwd, "tp", RING, -1)
    priors, scan_token = call(scan_kernel, [slices, TOKEN], 1, 1 << 20)(states)
    prior = lax.all_to_all(priors, BLOCKS, 0, 0, tiled=True).reshape(STATE)
    column_low, column_high = shift(column, "dp", 4, 1), shift(column, "dp", 4, -1)
    gain_row = gain.reshape(1, WIDTH)
    att, gated = call(norm_kernel, [(SQUARE, F32), (SQUARE, BF)], 5, 1 << 30)(
        queries, keys, values, gain_row, prior
    )
    relay = ((2, 128, WIDTH), BF)
    relay_low, relay_high = call(
        relay_rows_kernel, [relay, relay], 0, 0, 4, [pltpu.SemaphoreType.DMA((2,))], True
    )(fwd, bwd, column_low, column_high)
    fwd, bwd = tie((fwd, bwd), (scan_token,))
    chunks += [fwd, bwd]

    fwd, bwd = shift(fwd, "tp", RING, 1), shift(bwd, "tp", RING, -1)
    relay_low, relay_high = shift(relay_low, "dp", 4, 1), shift(relay_high, "dp", 4, -1)
    half = ((TOKENS // 2, WIDTH), BF)
    last_low, last_high, weight = call(
        turn_kernel, [half, half, ((4, 4, 128, WIDTH), BF)], 7, 1 << 20, 1
    )(gated, fwd, bwd, column, column_low, column_high, relay_low, relay_high)
    chunks += [fwd, bwd]
    last_low, last_high = shift(last_low, "tp", RING, 1), shift(last_high, "tp", RING, -1)
    weight_other = swap_cores(weight)

    wide = ((8, WIDTH, WIDTH), BF)
    partial_sum, parts, weight_last = call(
        early_kernel,
        [(SQUARE, F32), wide, ((2, WIDTH, WIDTH), BF)],
        3,
        1 << 33,
        7,
        [pltpu.VMEM((7, TOKENS, WIDTH), BF), pltpu.SemaphoreType.DMA((7,))],
    )(*chunks, gated, weight, weight_other)
    last, other = call(last_kernel, [(SQUARE, BF), ((4, WIDTH, WIDTH), BF)], 4, 1 << 29)(
        last_low, last_high, gated, parts
    )
    ga, send, grad_token = call(
        grad_kernel,
        [(SQUARE, BF), (STATE_GAIN, BF), TOKEN],
        7,
        1 << 30,
        0,
        [pltpu.VMEM(SQUARE, F32)],
    )(last_low, last_high, weight_last, partial_sum, queries, att, gain_row)
    quarter, eighth = ((4, WIDTH, 128), BF), ((2 * WIDTH, 128), BF)
    part, up, down, low, high = call(
        combine_kernel,
        [quarter, quarter, quarter, eighth, eighth],
        4,
        1 << 20,
        0,
        [pltpu.VMEM(SQUARE, BF)],
    )(grad_token, parts, swap_cores(other), last)
    total, after = call(row_back_kernel, [(STATE_GAIN, BF), (STATE, F32)], 4, 1 << 22)(
        send, *[shift(send, "dp", 4, -k) for k in (1, 2, 3)]
    )
    up, down = call(relay_kernel, [quarter, quarter], 4, 1 << 20, 1)(
        total, up, down, shift(low, "dp", 4, 1), shift(high, "dp", 4, -1)
    )
    query_grad, key_part, value_part, token = call(
        post_kernel, [(SQUARE, BF), (SQUARE, F32), (SQUARE, F32), TOKEN], 5, 1 << 31
    )(queries, keys, values, ga, prior)
    block = (WIDTH, 128)
    part, up, away, down = call(
        column_kernel,
        [(block, F32), (block, BF), (block, BF), (block, BF)],
        4,
        1 << 20,
        0,
        [pltpu.VMEM((4, WIDTH, 128), F32)],
    )(token, part, shift(up, "dp", 4, 1), shift(down, "dp", 4, -1))
    (weight_grad,) = call(sum_kernel, [((128, WIDTH), F32)], 4, 1 << 20)(
        part, shift(up, "y", 4, 1), shift(away, "y", 4, 2), shift(down, "y", 4, -1)
    )
    other = swap_cores(total)
    (both,) = call(pair_back_kernel, [(STATE_GAIN, BF)], 2, 1 << 22)(total, other)
    upper = [shift(both, "y", 4, -k) for k in (1, 2, 3)]
    key_grad, value_grad, gain_sum = call(
        final_kernel, [(SQUARE, BF), (SQUARE, BF), ((HEADS, HEAD_DIM), F32)], 10, 1 << 28, 1
    )(down, keys, values, key_part, value_part, after, other, both, *upper)
    gain_grad = gain_sum.reshape(WIDTH)
    return query_grad, key_grad, value_grad, gain_grad, weight_grad


def solution(mesh):
    grid = Mesh(mesh.devices.reshape(4, 2, RING, 4), ("y", "core", "tp", "dp"))
    rows = P(("y", "core", "dp"), "tp")
    return jax.shard_map(
        body,
        mesh=grid,
        in_specs=(rows, rows, rows, P("tp"), rows, rows),
        out_specs=(rows, rows, rows, P("tp"), rows),
        check_vma=False,
    )
```

```python
import math

import jax
import jax.numpy as jnp
from jax import lax
from jax.experimental import pallas as pl
from jax.experimental.pallas import tpu as pltpu
from jax.sharding import Mesh
from jax.sharding import PartitionSpec as P

HEAD_DIM = 128
HEADS = 4
TOKENS = 512
WIDTH = 512
RING = 8
EPS = 1e-06
SCALE = 1.0 / math.sqrt(16384.0)
BF = jnp.bfloat16
F32 = jnp.float32
PLANE = ("y", "dp")
BLOCKS = ("y", "core", "dp")
VMEM_LIMIT = 24 * 1024 * 1024
STATE = (HEADS * HEAD_DIM, HEAD_DIM)
STATE_GAIN = (HEADS * HEAD_DIM + 16, HEAD_DIM)
SQUARE = (TOKENS, WIDTH)
TOKEN = ((8, HEAD_DIM), jnp.float32)

NN = ((1,), (0,))
NT = ((1,), (1,))
TN = ((0,), (0,))


def dot(a, b, dims):
    return lax.dot_general(a, b, (dims, ((), ())), preferred_element_type=F32)


def span(h):
    return pl.ds(pl.multiple_of(h * HEAD_DIM, HEAD_DIM), HEAD_DIM)


def each(count, step, unroll=1):
    lax.fori_loop(0, count, lambda i, carry: (step(i), carry)[1], 0, unroll=unroll)


def causal_mask():
    rows = lax.broadcasted_iota(jnp.int32, (TOKENS, TOKENS), 0)
    cols = lax.broadcasted_iota(jnp.int32, (TOKENS, TOKENS), 1)
    return rows >= cols


def call(kernel, out, n_in, flops, any_in=0, scratch=(), any_out=False):
    vmem = pl.BlockSpec(memory_space=pltpu.VMEM)
    anys = pl.BlockSpec(memory_space=pl.ANY)
    return pl.pallas_call(
        kernel,
        out_shape=tuple(jax.ShapeDtypeStruct(s, d) for s, d in out),
        in_specs=[anys] * any_in + [vmem] * n_in,
        out_specs=tuple(anys if any_out else vmem for _ in out),
        scratch_shapes=scratch,
        compiler_params=pltpu.CompilerParams(vmem_limit_bytes=VMEM_LIMIT),
        cost_estimate=pl.CostEstimate(flops=flops, bytes_accessed=4 << 20, transcendentals=0),
    )


def state_kernel(k_ref, v_ref, out_ref, token_ref):
    token_ref[...] = jnp.zeros(TOKEN[0], F32)

    def step(h):
        state = dot(k_ref[:, span(h)], v_ref[:, span(h)], TN).astype(BF)
        out_ref[pl.ds(h * 8, 8)] = state.reshape(8, 16, HEAD_DIM)

    each(HEADS, step)


def scan_kernel(in_ref, out_ref, token_ref):
    token_ref[...] = jnp.zeros(TOKEN[0], F32)
    total = jnp.zeros((16, HEAD_DIM), F32)
    for c in range(32):
        out_ref[c] = total.astype(BF)
        total = total + in_ref[c].astype(F32)


def when(flag):
    return jnp.where(flag, 1.0, 0.0).astype(F32)


def norm_kernel(q_ref, k_ref, v_ref, gain_ref, prior_ref, att_ref, gated_ref):
    mask = causal_mask()

    def step(h):
        cols = span(h)
        scores = dot(q_ref[:, cols], k_ref[:, cols], NT)
        scores = jnp.where(mask, scores, 0.0).astype(BF)
        att = dot(scores, v_ref[:, cols], NN) + dot(q_ref[:, cols], prior_ref[cols], NN)
        att_ref[:, cols] = att
        inverse = lax.rsqrt(jnp.mean(att * att, axis=-1, keepdims=True) + EPS)
        gated = (att * inverse * gain_ref[:, cols]).astype(BF)
        gated_ref[cols, :] = gated.T

    each(HEADS, step, 4)


def is_same():
    return lax.rem(lax.axis_index("tp"), 2) == lax.axis_index("core")


def row_of(k):
    return lax.div(lax.rem(lax.axis_index("tp") + k + RING, RING), 2)


EVENS = (0, 2, -2, 4)
ODDS = (1, -1, 3, -3)


ORDER = (0, 2, -2, 1, -1, 3, -3)


def early_kernel(*refs):
    own, f1, b1, f2, b2, f3, b3, gated_ref, wm_ref, wo_ref = refs[:10]
    sum_ref, part_ref, weight_ref, rows, sems = refs[10:]
    copies = []
    for n, ref in enumerate((own, b2, f2, b1, f1, b3, f3)):
        copies.append(pltpu.make_async_copy(ref, rows.at[n], sems.at[n]))
    for c in copies:
        c.start()
    for c in copies:
        c.wait()
    sum_ref[...] = jnp.zeros(SQUARE, F32)
    same = is_same()

    def offset(n):
        k = jnp.int32(ORDER[-1])
        for i in range(len(ORDER) - 1):
            k = jnp.where(n == i, ORDER[i], k)
        return k

    def fetch(even, k, slot):
        mine = jnp.logical_not(jnp.logical_xor(same, even))
        y = row_of(k)

        @pl.when(mine)
        def _():
            weight_ref[slot] = wm_ref[y].reshape(SQUARE)

        @pl.when(jnp.logical_not(mine))
        def _():
            weight_ref[slot] = wo_ref[y].reshape(SQUARE)

    def part(n):
        part_ref[jnp.where(n < 3, n, n + 1)] = dot(gated_ref[...], rows[n], NN).astype(BF)

    def step(i):
        n = 2 * i
        for m in range(2):
            fetch(n + m < 3, offset(n + m), m)
            part(n + m)
        first = dot(rows[n], weight_ref[0], NN)
        sum_ref[...] += first + dot(rows[n + 1], weight_ref[1], NN)

    each(3, step)
    fetch(jnp.bool_(False), jnp.int32(ORDER[6]), 0)
    part(jnp.int32(6))
    sum_ref[...] += dot(rows[6], weight_ref[0], NN)
    fetch(jnp.bool_(True), jnp.int32(4), 0)


def last_kernel(low_ref, high_ref, gated_ref, part_ref, last_ref, other_ref):
    half = TOKENS // 2
    last = dot(gated_ref[:, 0:half], low_ref[...], NN)
    last_ref[...] = (last + dot(gated_ref[:, half:TOKENS], high_ref[...], NN)).astype(BF)
    base = jnp.where(is_same(), 4, 0)

    def step(s):
        other_ref[s] = part_ref[base + s]

    each(3, step)

    @pl.when(is_same())
    def _():
        other_ref[3] = part_ref[7]

    @pl.when(jnp.logical_not(is_same()))
    def _():
        other_ref[3] = last_ref[...]


def grad_kernel(
    low_ref, high_ref, weight_ref, sum_ref, q_ref, att_ref, gain_ref, ga_ref, send_ref, token_ref, acc
):
    token_ref[...] = jnp.zeros(TOKEN[0], F32)
    half = TOKENS // 2
    acc[0:half] = sum_ref[0:half] + dot(low_ref[...], weight_ref[0], NN)
    acc[half:TOKENS] = sum_ref[half:TOKENS] + dot(high_ref[...], weight_ref[0], NN)
    grad_rows(acc, q_ref, att_ref, gain_ref, ga_ref, send_ref)


def combine_kernel(
    after_ref, part_ref, got_ref, last_ref, own_ref, up_ref, down_ref, low_ref, high_ref, rows
):
    place = lax.axis_index("dp")
    same = is_same()
    base = jnp.where(same, 0, 4)

    def step(s):
        late = jnp.logical_and(same, s == 3)

        @pl.when(late)
        def _():
            rows[...] = (last_ref[...].astype(F32) + got_ref[s].astype(F32)).astype(BF)

        @pl.when(jnp.logical_not(late))
        def _():
            rows[...] = (part_ref[base + s].astype(F32) + got_ref[s].astype(F32)).astype(BF)

        blocks = []
        for d in range(4):
            start = pl.multiple_of(lax.rem(place + d, 4) * 128, 128)
            blocks.append(rows[:, pl.ds(start, 128)])
        own_ref[s], up_ref[s], down_ref[s] = blocks[0], blocks[1], blocks[3]
        at = pl.ds(pl.multiple_of(s * 256, 256), 256)
        low_ref[at], high_ref[at] = blocks[2][0:256], blocks[2][256:512]

    each(4, step)


def pack_kernel(
    after1_ref, after2_ref, own_ref, r1_ref, r2_ref, r3_ref, out_ref, token_out, token, sems
):
    token[...] = jnp.zeros(TOKEN[0], F32)
    y = lax.axis_index("y")
    copies = [pltpu.make_async_copy(token, token_out, sems.at[4])]
    for k, ref in enumerate((own_ref, r1_ref, r2_ref, r3_ref)):
        copies.append(pltpu.make_async_copy(ref, out_ref.at[lax.rem(y + 4 - k, 4)], sems.at[k]))
    for c in copies:
        c.start()
    for c in copies:
        c.wait()


def relay_rows_kernel(after1_ref, after2_ref, low_ref, high_ref, low_out, high_out, sems):
    low = pltpu.make_async_copy(low_ref.at[0:2], low_out, sems.at[0])
    high = pltpu.make_async_copy(high_ref.at[2:4], high_out, sems.at[1])
    low.start()
    high.start()
    low.wait()
    high.wait()


def turn_kernel(
    after_ref, fwd_ref, bwd_ref, own_ref, low_ref, high_ref, far_low_ref, far_high_ref,
    fwd_out, bwd_out, out_ref,
):
    fwd_out[...] = fwd_ref[0 : TOKENS // 2]
    bwd_out[...] = bwd_ref[TOKENS // 2 : TOKENS]
    x = lax.axis_index("dp")
    for k, ref in ((0, own_ref), (3, low_ref), (1, high_ref)):
        for y in range(4):
            out_ref[y, lax.rem(x + k, 4)] = ref[y]
    for y in range(2):
        out_ref[y, lax.rem(x + 2, 4)] = far_low_ref[y]
        out_ref[2 + y, lax.rem(x + 2, 4)] = far_high_ref[y]


def tie(values, deps):
    def kernel(*refs):
        pass

    n = len(values)
    anys = pl.BlockSpec(memory_space=pl.ANY)
    return pl.pallas_call(
        kernel,
        out_shape=tuple(jax.ShapeDtypeStruct(v.shape, v.dtype) for v in values),
        in_specs=[anys] * (n + len(deps)),
        out_specs=(anys,) * n,
        input_output_aliases={i: i for i in range(n)},
        compiler_params=pltpu.CompilerParams(vmem_limit_bytes=1 << 20),
        cost_estimate=pl.CostEstimate(flops=0, bytes_accessed=0, transcendentals=0),
    )(*values, *deps)


def relay_kernel(after_ref, up_ref, down_ref, low_ref, high_ref, up_out, down_out):
    def step(y):
        rows = pl.ds(pl.multiple_of(y * 256, 256), 256)
        up_out[y, 0:256] = (up_ref[y, 0:256].astype(F32) + low_ref[rows].astype(F32)).astype(BF)
        up_out[y, 256:512] = up_ref[y, 256:512]
        down_out[y, 0:256] = down_ref[y, 0:256]
        low = down_ref[y, 256:512].astype(F32) + high_ref[rows].astype(F32)
        down_out[y, 256:512] = low.astype(BF)

    each(4, step)


def column_kernel(after_ref, own_ref, a_ref, b_ref, own_out, up_out, far_out, down_out, rows):
    same = is_same()

    def step(s):
        k = jnp.where(s == 3, 4, jnp.where(s == 2, -2, s * 2))
        odd = jnp.where(s == 3, -3, jnp.where(s == 2, 3, 1 - 2 * s))
        y = row_of(jnp.where(same, k, odd))
        total = own_ref[s].astype(F32) + a_ref[s].astype(F32) + b_ref[s].astype(F32)
        rows[lax.rem(y + 4 - lax.axis_index("y"), 4)] = total

    each(4, step)
    own_out[...] = rows[0]
    up_out[...] = rows[1].astype(BF)
    far_out[...] = rows[2].astype(BF)
    down_out[...] = rows[3].astype(BF)


def grad_rows(own_ref, q_ref, att_ref, gain_ref, ga_ref, send_ref):
    base = HEADS * HEAD_DIM
    rows = lax.broadcasted_iota(jnp.int32, (16, HEAD_DIM), 0)

    def step(h, sums):
        att = att_ref[:, span(h)]
        inverse = lax.rsqrt(jnp.mean(att * att, axis=-1, keepdims=True) + EPS)
        normed = att * inverse
        grad = own_ref[:, span(h)]
        part = jnp.sum(grad * normed, axis=0, keepdims=True)
        high = part.astype(BF).astype(F32)
        sums = sums + jnp.where(rows == h, high, 0.0) + jnp.where(rows == 4 + h, part - high, 0.0)
        grad = grad * gain_ref[:, span(h)]
        grad = (grad - normed * jnp.mean(grad * normed, axis=-1, keepdims=True)) * inverse
        grad = grad.astype(BF)
        ga_ref[:, span(h)] = grad
        send_ref[span(h)] = dot(q_ref[:, span(h)], grad, TN).astype(BF)
        return sums

    sums = lax.fori_loop(0, HEADS, step, jnp.zeros((16, HEAD_DIM), F32), unroll=2)
    send_ref[base:] = sums.astype(BF)


def resum(parts):
    total = sum(p.astype(F32) for p in parts)
    gain = total[0:4] + total[4:8]
    high = gain.astype(BF).astype(F32)
    return jnp.concatenate([high, gain - high, jnp.zeros((8, HEAD_DIM), F32)], axis=0)


def row_back_kernel(own_ref, r1_ref, r2_ref, r3_ref, total_ref, after_ref):
    x = lax.axis_index("dp")
    base = HEADS * HEAD_DIM
    r1, r2, r3 = (r[0:base].astype(F32) for r in (r1_ref, r2_ref, r3_ref))
    after_ref[...] = r1 * when(x <= 2) + r2 * when(x <= 1) + r3 * when(x <= 0)
    total_ref[0:base] = (own_ref[0:base].astype(F32) + r1 + r2 + r3).astype(BF)
    total_ref[base:] = resum([r[base:] for r in (own_ref, r1_ref, r2_ref, r3_ref)]).astype(BF)


def pair_back_kernel(total_ref, other_ref, out_ref):
    base = HEADS * HEAD_DIM
    out_ref[0:base] = (total_ref[0:base].astype(F32) + other_ref[0:base].astype(F32)).astype(BF)
    out_ref[base:] = resum([total_ref[base:], other_ref[base:]]).astype(BF)


def post_kernel(q_ref, k_ref, v_ref, ga_ref, prior_ref, qg_ref, kp_ref, vp_ref, token_ref):
    token_ref[...] = jnp.zeros(TOKEN[0], F32)
    mask = causal_mask()

    def step(h):
        cols = span(h)
        q, k, v, ga = q_ref[:, cols], k_ref[:, cols], v_ref[:, cols], ga_ref[:, cols]
        scores = jnp.where(mask, dot(q, k, NT), 0.0).astype(BF)
        vp_ref[:, cols] = dot(scores, ga, TN)
        back = jnp.where(mask, dot(ga, v, NT), 0.0).astype(BF)
        qg_ref[:, cols] = (dot(back, k, NN) + dot(ga, prior_ref[cols], NT)).astype(BF)
        kp_ref[:, cols] = dot(back, q, TN)

    each(HEADS, step)


def final_kernel(
    after_last_ref, k_ref, v_ref, kp_ref, vp_ref, after_ref, other_ref, own, u1, u2, u3, kg_ref, vg_ref, gain_ref
):
    base = HEADS * HEAD_DIM
    y = lax.axis_index("y")
    first = when(lax.axis_index("core") == 0)

    def step(h):
        cols = span(h)
        later = after_ref[cols] + other_ref[cols].astype(F32) * first
        later = later + u1[cols].astype(F32) * when(y <= 2) + u2[cols].astype(F32) * when(y <= 1)
        later = (later + u3[cols].astype(F32) * when(y <= 0)).astype(BF)
        kg_ref[:, cols] = (kp_ref[:, cols] + dot(v_ref[:, cols], later, NT)).astype(BF)
        vg_ref[:, cols] = (vp_ref[:, cols] + dot(k_ref[:, cols], later, NN)).astype(BF)

    each(HEADS, step, 2)
    gain = resum([r[base:] for r in (own, u1, u2, u3)])
    gain_ref[...] = (gain[0:4] + gain[4:8]) * SCALE


def sum_kernel(own_ref, r1_ref, r2_ref, r3_ref, out_ref):
    total = own_ref[...]
    for ref in (r1_ref, r2_ref, r3_ref):
        total = total + ref[...].astype(F32)
    out_ref[...] = (total * SCALE).T


def shift(x, axis, size, k, wrap=True):
    pairs = [(i, (i + k) % size) for i in range(size) if wrap or 0 <= i + k < size]
    return lax.ppermute(x, axis, pairs)


def swap_cores(x):
    return lax.ppermute(x, "core", [(0, 1), (1, 0)])


def body(queries, keys, values, gain, out_weight, out_cotangent):
    own = out_cotangent
    fwd, bwd = shift(own, "tp", RING, 1), shift(own, "tp", RING, -1)
    slices = ((32, 16, HEAD_DIM), BF)
    state, state_token = call(state_kernel, [slices, TOKEN], 2, 1 << 27)(keys, values)
    states = lax.all_to_all(state, BLOCKS, 0, 0, tiled=True)
    others = [shift(out_weight, "y", 4, k) for k in (1, 2, 3)]
    column, column_token = call(
        pack_kernel,
        [((4, 128, WIDTH), BF), TOKEN],
        0,
        1 << 20,
        6,
        [pltpu.VMEM(*TOKEN), pltpu.SemaphoreType.DMA((5,))],
        True,
    )(fwd, bwd, out_weight, *others)
    fwd, bwd = tie((fwd, bwd), (state_token, column_token))
    chunks = [own, fwd, bwd]

    fwd, bwd = shift(fwd, "tp", RING, 1), shift(bwd, "tp", RING, -1)
    priors, scan_token = call(scan_kernel, [slices, TOKEN], 1, 1 << 20)(states)
    prior = lax.all_to_all(priors, BLOCKS, 0, 0, tiled=True).reshape(STATE)
    column_low, column_high = shift(column, "dp", 4, 1), shift(column, "dp", 4, -1)
    gain_row = gain.reshape(1, WIDTH)
    att, gated = call(norm_kernel, [(SQUARE, F32), (SQUARE, BF)], 5, 1 << 30)(
        queries, keys, values, gain_row, prior
    )
    relay = ((2, 128, WIDTH), BF)
    relay_low, relay_high = call(
        relay_rows_kernel, [relay, relay], 0, 0, 4, [pltpu.SemaphoreType.DMA((2,))], True
    )(fwd, bwd, column_low, column_high)
    fwd, bwd = tie((fwd, bwd), (scan_token,))
    chunks += [fwd, bwd]

    fwd, bwd = shift(fwd, "tp", RING, 1), shift(bwd, "tp", RING, -1)
    relay_low, relay_high = shift(relay_low, "dp", 4, 1), shift(relay_high, "dp", 4, -1)
    half = ((TOKENS // 2, WIDTH), BF)
    last_low, last_high, weight = call(
        turn_kernel, [half, half, ((4, 4, 128, WIDTH), BF)], 7, 1 << 20, 1
    )(gated, fwd, bwd, column, column_low, column_high, relay_low, relay_high)
    chunks += [fwd, bwd]
    last_low, last_high = shift(last_low, "tp", RING, 1), shift(last_high, "tp", RING, -1)
    weight_other = swap_cores(weight)

    wide = ((8, WIDTH, WIDTH), BF)
    partial_sum, parts, weight_last = call(
        early_kernel,
        [(SQUARE, F32), wide, ((2, WIDTH, WIDTH), BF)],
        3,
        1 << 33,
        7,
        [pltpu.VMEM((7, TOKENS, WIDTH), BF), pltpu.SemaphoreType.DMA((7,))],
    )(*chunks, gated, weight, weight_other)
    last, other = call(last_kernel, [(SQUARE, BF), ((4, WIDTH, WIDTH), BF)], 4, 1 << 29)(
        last_low, last_high, gated, parts
    )
    ga, send, grad_token = call(
        grad_kernel,
        [(SQUARE, BF), (STATE_GAIN, BF), TOKEN],
        7,
        1 << 30,
        0,
        [pltpu.VMEM(SQUARE, F32)],
    )(last_low, last_high, weight_last, partial_sum, queries, att, gain_row)
    quarter, eighth = ((4, WIDTH, 128), BF), ((2 * WIDTH, 128), BF)
    part, up, down, low, high = call(
        combine_kernel,
        [quarter, quarter, quarter, eighth, eighth],
        4,
        1 << 20,
        0,
        [pltpu.VMEM(SQUARE, BF)],
    )(grad_token, parts, swap_cores(other), last)
    total, after = call(row_back_kernel, [(STATE_GAIN, BF), (STATE, F32)], 4, 1 << 22)(
        send, *[shift(send, "dp", 4, -k) for k in (1, 2, 3)]
    )
    up, down = call(relay_kernel, [quarter, quarter], 4, 1 << 20, 1)(
        total, up, down, shift(low, "dp", 4, 1), shift(high, "dp", 4, -1)
    )
    query_grad, key_part, value_part, token = call(
        post_kernel, [(SQUARE, BF), (SQUARE, F32), (SQUARE, F32), TOKEN], 5, 1 << 31
    )(queries, keys, values, ga, prior)
    block = (WIDTH, 128)
    part, up, away, down = call(
        column_kernel,
        [(block, F32), (block, BF), (block, BF), (block, BF)],
        4,
        1 << 20,
        0,
        [pltpu.VMEM((4, WIDTH, 128), F32)],
    )(token, part, shift(up, "dp", 4, 1), shift(down, "dp", 4, -1))
    (weight_grad,) = call(sum_kernel, [((128, WIDTH), F32)], 4, 1 << 20)(
        part, shift(up, "y", 4, 1), shift(away, "y", 4, 2), shift(down, "y", 4, -1)
    )
    other = swap_cores(total)
    (both,) = call(pair_back_kernel, [(STATE_GAIN, BF)], 2, 1 << 22)(total, other)
    upper = [shift(both, "y", 4, -k) for k in (1, 2, 3)]
    key_grad, value_grad, gain_sum = call(
        final_kernel, [(SQUARE, BF), (SQUARE, BF), ((HEADS, HEAD_DIM), F32)], 10, 1 << 28, 1
    )(down, keys, values, key_part, value_part, after, other, both, *upper)
    gain_grad = gain_sum.reshape(WIDTH)
    return query_grad, key_grad, value_grad, gain_grad, weight_grad


def solution(mesh):
    grid = Mesh(mesh.devices.reshape(4, 2, RING, 4), ("y", "core", "tp", "dp"))
    rows = P(("y", "core", "dp"), "tp")
    return jax.shard_map(
        body,
        mesh=grid,
        in_specs=(rows, rows, rows, P("tp"), rows, rows),
        out_specs=(rows, rows, rows, P("tp"), rows),
        check_vma=False,
    )
```

```python
import math

import jax
import jax.numpy as jnp
from jax import lax
from jax.experimental import pallas as pl
from jax.experimental.pallas import tpu as pltpu
from jax.sharding import Mesh
from jax.sharding import PartitionSpec as P

HEAD_DIM = 128
HEADS = 4
TOKENS = 512
WIDTH = 512
RING = 8
EPS = 1e-06
SCALE = 1.0 / math.sqrt(16384.0)
BF = jnp.bfloat16
F32 = jnp.float32
PLANE = ("y", "dp")
BLOCKS = ("y", "core", "dp")
VMEM_LIMIT = 24 * 1024 * 1024
STATE = (HEADS * HEAD_DIM, HEAD_DIM)
STATE_GAIN = (HEADS * HEAD_DIM + 16, HEAD_DIM)
SQUARE = (TOKENS, WIDTH)
TOKEN = ((8, HEAD_DIM), jnp.float32)

NN = ((1,), (0,))
NT = ((1,), (1,))
TN = ((0,), (0,))


def dot(a, b, dims):
    return lax.dot_general(a, b, (dims, ((), ())), preferred_element_type=F32)


def span(h):
    return pl.ds(pl.multiple_of(h * HEAD_DIM, HEAD_DIM), HEAD_DIM)


def each(count, step, unroll=1):
    lax.fori_loop(0, count, lambda i, carry: (step(i), carry)[1], 0, unroll=unroll)


def causal_mask():
    rows = lax.broadcasted_iota(jnp.int32, (TOKENS, TOKENS), 0)
    cols = lax.broadcasted_iota(jnp.int32, (TOKENS, TOKENS), 1)
    return rows >= cols


def call(kernel, out, n_in, flops, any_in=0, scratch=(), any_out=False):
    vmem = pl.BlockSpec(memory_space=pltpu.VMEM)
    anys = pl.BlockSpec(memory_space=pl.ANY)
    return pl.pallas_call(
        kernel,
        out_shape=tuple(jax.ShapeDtypeStruct(s, d) for s, d in out),
        in_specs=[anys] * any_in + [vmem] * n_in,
        out_specs=tuple(anys if any_out else vmem for _ in out),
        scratch_shapes=scratch,
        compiler_params=pltpu.CompilerParams(vmem_limit_bytes=VMEM_LIMIT),
        cost_estimate=pl.CostEstimate(flops=flops, bytes_accessed=4 << 20, transcendentals=0),
    )


def state_kernel(k_ref, v_ref, out_ref, token_ref):
    token_ref[...] = jnp.zeros(TOKEN[0], F32)

    def step(h):
        state = dot(k_ref[:, span(h)], v_ref[:, span(h)], TN).astype(BF)
        out_ref[pl.ds(h * 8, 8)] = state.reshape(8, 16, HEAD_DIM)

    each(HEADS, step)


def scan_kernel(in_ref, out_ref, token_ref):
    token_ref[...] = jnp.zeros(TOKEN[0], F32)
    total = jnp.zeros((16, HEAD_DIM), F32)
    for c in range(32):
        out_ref[c] = total.astype(BF)
        total = total + in_ref[c].astype(F32)


def when(flag):
    return jnp.where(flag, 1.0, 0.0).astype(F32)


def norm_kernel(q_ref, k_ref, v_ref, gain_ref, prior_ref, att_ref, gated_ref):
    mask = causal_mask()

    def step(h):
        cols = span(h)
        scores = dot(q_ref[:, cols], k_ref[:, cols], NT)
        scores = jnp.where(mask, scores, 0.0).astype(BF)
        att = dot(scores, v_ref[:, cols], NN) + dot(q_ref[:, cols], prior_ref[cols], NN)
        att_ref[:, cols] = att
        inverse = lax.rsqrt(jnp.mean(att * att, axis=-1, keepdims=True) + EPS)
        gated = (att * inverse * gain_ref[:, cols]).astype(BF)
        gated_ref[cols, :] = gated.T

    each(HEADS, step, 4)


def is_same():
    return lax.rem(lax.axis_index("tp"), 2) == lax.axis_index("core")


def row_of(k):
    return lax.div(lax.rem(lax.axis_index("tp") + k + RING, RING), 2)


EVENS = (0, 2, -2, 4)
ODDS = (1, -1, 3, -3)


ORDER = (0, 2, -2, 1, -1, 3, -3)


def early_kernel(*refs):
    own, f1, b1, f2, b2, f3, b3, gated_ref, wm_ref, wo_ref = refs[:10]
    sum_ref, part_ref, weight_ref, rows, sems = refs[10:]
    copies = []
    for n, ref in enumerate((own, b2, f2, b1, f1, b3, f3)):
        copies.append(pltpu.make_async_copy(ref, rows.at[n], sems.at[n]))
    for c in copies:
        c.start()
    for c in copies:
        c.wait()
    sum_ref[...] = jnp.zeros(SQUARE, F32)
    same = is_same()

    def offset(n):
        k = jnp.int32(ORDER[-1])
        for i in range(len(ORDER) - 1):
            k = jnp.where(n == i, ORDER[i], k)
        return k

    def fetch(even, k, slot):
        mine = jnp.logical_not(jnp.logical_xor(same, even))
        y = row_of(k)

        @pl.when(mine)
        def _():
            weight_ref[slot] = wm_ref[y].reshape(SQUARE)

        @pl.when(jnp.logical_not(mine))
        def _():
            weight_ref[slot] = wo_ref[y].reshape(SQUARE)

    def part(n):
        part_ref[jnp.where(n < 3, n, n + 1)] = dot(gated_ref[...], rows[n], NN).astype(BF)

    def step(i):
        n = 2 * i
        for m in range(2):
            fetch(n + m < 3, offset(n + m), m)
            part(n + m)
        first = dot(rows[n], weight_ref[0], NN)
        sum_ref[...] += first + dot(rows[n + 1], weight_ref[1], NN)

    each(3, step)
    fetch(jnp.bool_(False), jnp.int32(ORDER[6]), 0)
    part(jnp.int32(6))
    sum_ref[...] += dot(rows[6], weight_ref[0], NN)
    fetch(jnp.bool_(True), jnp.int32(4), 0)


def last_kernel(low_ref, high_ref, gated_ref, part_ref, last_ref, other_ref):
    half = TOKENS // 2
    last = dot(gated_ref[:, 0:half], low_ref[...], NN)
    last_ref[...] = (last + dot(gated_ref[:, half:TOKENS], high_ref[...], NN)).astype(BF)
    base = jnp.where(is_same(), 4, 0)

    def step(s):
        other_ref[s] = part_ref[base + s]

    each(3, step)

    @pl.when(is_same())
    def _():
        other_ref[3] = part_ref[7]

    @pl.when(jnp.logical_not(is_same()))
    def _():
        other_ref[3] = last_ref[...]


def grad_kernel(
    low_ref, high_ref, weight_ref, sum_ref, q_ref, att_ref, gain_ref, ga_ref, send_ref, token_ref, acc
):
    token_ref[...] = jnp.zeros(TOKEN[0], F32)
    half = TOKENS // 2
    acc[0:half] = sum_ref[0:half] + dot(low_ref[...], weight_ref[0], NN)
    acc[half:TOKENS] = sum_ref[half:TOKENS] + dot(high_ref[...], weight_ref[0], NN)
    grad_rows(acc, q_ref, att_ref, gain_ref, ga_ref, send_ref)


def combine_kernel(
    after_ref, part_ref, got_ref, last_ref, own_ref, up_ref, down_ref, low_ref, high_ref, rows
):
    place = lax.axis_index("dp")
    same = is_same()
    base = jnp.where(same, 0, 4)

    def step(s):
        late = jnp.logical_and(same, s == 3)

        @pl.when(late)
        def _():
            rows[...] = (last_ref[...].astype(F32) + got_ref[s].astype(F32)).astype(BF)

        @pl.when(jnp.logical_not(late))
        def _():
            rows[...] = (part_ref[base + s].astype(F32) + got_ref[s].astype(F32)).astype(BF)

        blocks = []
        for d in range(4):
            start = pl.multiple_of(lax.rem(place + d, 4) * 128, 128)
            blocks.append(rows[:, pl.ds(start, 128)])
        own_ref[s], up_ref[s], down_ref[s] = blocks[0], blocks[1], blocks[3]
        at = pl.ds(pl.multiple_of(s * 256, 256), 256)
        low_ref[at], high_ref[at] = blocks[2][0:256], blocks[2][256:512]

    each(4, step)


def pack_kernel(
    after1_ref, after2_ref, own_ref, r1_ref, r2_ref, r3_ref, out_ref, token_out, token, sems
):
    token[...] = jnp.zeros(TOKEN[0], F32)
    y = lax.axis_index("y")
    copies = [pltpu.make_async_copy(token, token_out, sems.at[4])]
    for k, ref in enumerate((own_ref, r1_ref, r2_ref, r3_ref)):
        copies.append(pltpu.make_async_copy(ref, out_ref.at[lax.rem(y + 4 - k, 4)], sems.at[k]))
    for c in copies:
        c.start()
    for c in copies:
        c.wait()


def relay_rows_kernel(after1_ref, after2_ref, low_ref, high_ref, low_out, high_out, sems):
    low = pltpu.make_async_copy(low_ref.at[0:2], low_out, sems.at[0])
    high = pltpu.make_async_copy(high_ref.at[2:4], high_out, sems.at[1])
    low.start()
    high.start()
    low.wait()
    high.wait()


def turn_kernel(
    after_ref, fwd_ref, bwd_ref, own_ref, low_ref, high_ref, far_low_ref, far_high_ref,
    fwd_out, bwd_out, out_ref,
):
    fwd_out[...] = fwd_ref[0 : TOKENS // 2]
    bwd_out[...] = bwd_ref[TOKENS // 2 : TOKENS]
    x = lax.axis_index("dp")
    for k, ref in ((0, own_ref), (3, low_ref), (1, high_ref)):
        for y in range(4):
            out_ref[y, lax.rem(x + k, 4)] = ref[y]
    for y in range(2):
        out_ref[y, lax.rem(x + 2, 4)] = far_low_ref[y]
        out_ref[2 + y, lax.rem(x + 2, 4)] = far_high_ref[y]


def tie(values, deps):
    def kernel(*refs):
        pass

    n = len(values)
    anys = pl.BlockSpec(memory_space=pl.ANY)
    return pl.pallas_call(
        kernel,
        out_shape=tuple(jax.ShapeDtypeStruct(v.shape, v.dtype) for v in values),
        in_specs=[anys] * (n + len(deps)),
        out_specs=(anys,) * n,
        input_output_aliases={i: i for i in range(n)},
        compiler_params=pltpu.CompilerParams(vmem_limit_bytes=1 << 20),
        cost_estimate=pl.CostEstimate(flops=0, bytes_accessed=0, transcendentals=0),
    )(*values, *deps)


def relay_kernel(after_ref, up_ref, down_ref, low_ref, high_ref, up_out, down_out):
    def step(y):
        rows = pl.ds(pl.multiple_of(y * 256, 256), 256)
        up_out[y, 0:256] = (up_ref[y, 0:256].astype(F32) + low_ref[rows].astype(F32)).astype(BF)
        up_out[y, 256:512] = up_ref[y, 256:512]
        down_out[y, 0:256] = down_ref[y, 0:256]
        low = down_ref[y, 256:512].astype(F32) + high_ref[rows].astype(F32)
        down_out[y, 256:512] = low.astype(BF)

    each(4, step)


def column_kernel(after_ref, own_ref, a_ref, b_ref, own_out, up_out, far_out, down_out, rows):
    same = is_same()

    def step(s):
        k = jnp.where(s == 3, 4, jnp.where(s == 2, -2, s * 2))
        odd = jnp.where(s == 3, -3, jnp.where(s == 2, 3, 1 - 2 * s))
        y = row_of(jnp.where(same, k, odd))
        total = own_ref[s].astype(F32) + a_ref[s].astype(F32) + b_ref[s].astype(F32)
        rows[lax.rem(y + 4 - lax.axis_index("y"), 4)] = total

    each(4, step)
    own_out[...] = rows[0]
    up_out[...] = rows[1].astype(BF)
    far_out[...] = rows[2].astype(BF)
    down_out[...] = rows[3].astype(BF)


def grad_rows(own_ref, q_ref, att_ref, gain_ref, ga_ref, send_ref):
    base = HEADS * HEAD_DIM
    rows = lax.broadcasted_iota(jnp.int32, (16, HEAD_DIM), 0)

    def step(h, sums):
        att = att_ref[:, span(h)]
        inverse = lax.rsqrt(jnp.mean(att * att, axis=-1, keepdims=True) + EPS)
        normed = att * inverse
        grad = own_ref[:, span(h)]
        part = jnp.sum(grad * normed, axis=0, keepdims=True)
        high = part.astype(BF).astype(F32)
        sums = sums + jnp.where(rows == h, high, 0.0) + jnp.where(rows == 4 + h, part - high, 0.0)
        grad = grad * gain_ref[:, span(h)]
        grad = (grad - normed * jnp.mean(grad * normed, axis=-1, keepdims=True)) * inverse
        grad = grad.astype(BF)
        ga_ref[:, span(h)] = grad
        send_ref[span(h)] = dot(q_ref[:, span(h)], grad, TN).astype(BF)
        return sums

    sums = lax.fori_loop(0, HEADS, step, jnp.zeros((16, HEAD_DIM), F32), unroll=2)
    send_ref[base:] = sums.astype(BF)


def resum(parts):
    total = sum(p.astype(F32) for p in parts)
    gain = total[0:4] + total[4:8]
    high = gain.astype(BF).astype(F32)
    return jnp.concatenate([high, gain - high, jnp.zeros((8, HEAD_DIM), F32)], axis=0)


def row_back_kernel(own_ref, r1_ref, r2_ref, r3_ref, total_ref, after_ref):
    x = lax.axis_index("dp")
    base = HEADS * HEAD_DIM
    r1, r2, r3 = (r[0:base].astype(F32) for r in (r1_ref, r2_ref, r3_ref))
    after_ref[...] = r1 * when(x <= 2) + r2 * when(x <= 1) + r3 * when(x <= 0)
    total_ref[0:base] = (own_ref[0:base].astype(F32) + r1 + r2 + r3).astype(BF)
    total_ref[base:] = resum([r[base:] for r in (own_ref, r1_ref, r2_ref, r3_ref)]).astype(BF)


def pair_back_kernel(total_ref, other_ref, out_ref):
    base = HEADS * HEAD_DIM
    out_ref[0:base] = (total_ref[0:base].astype(F32) + other_ref[0:base].astype(F32)).astype(BF)
    out_ref[base:] = resum([total_ref[base:], other_ref[base:]]).astype(BF)


def post_kernel(q_ref, k_ref, v_ref, ga_ref, prior_ref, qg_ref, kp_ref, vp_ref, token_ref):
    token_ref[...] = jnp.zeros(TOKEN[0], F32)
    mask = causal_mask()

    def step(h):
        cols = span(h)
        q, k, v, ga = q_ref[:, cols], k_ref[:, cols], v_ref[:, cols], ga_ref[:, cols]
        scores = jnp.where(mask, dot(q, k, NT), 0.0).astype(BF)
        vp_ref[:, cols] = dot(scores, ga, TN)
        back = jnp.where(mask, dot(ga, v, NT), 0.0).astype(BF)
        qg_ref[:, cols] = (dot(back, k, NN) + dot(ga, prior_ref[cols], NT)).astype(BF)
        kp_ref[:, cols] = dot(back, q, TN)

    each(HEADS, step)


def final_kernel(
    after_last_ref, k_ref, v_ref, kp_ref, vp_ref, after_ref, other_ref, own, u1, u2, u3, kg_ref, vg_ref, gain_ref
):
    base = HEADS * HEAD_DIM
    y = lax.axis_index("y")
    first = when(lax.axis_index("core") == 0)

    def step(h):
        cols = span(h)
        later = after_ref[cols] + other_ref[cols].astype(F32) * first
        later = later + u1[cols].astype(F32) * when(y <= 2) + u2[cols].astype(F32) * when(y <= 1)
        later = (later + u3[cols].astype(F32) * when(y <= 0)).astype(BF)
        kg_ref[:, cols] = (kp_ref[:, cols] + dot(v_ref[:, cols], later, NT)).astype(BF)
        vg_ref[:, cols] = (vp_ref[:, cols] + dot(k_ref[:, cols], later, NN)).astype(BF)

    each(HEADS, step, 2)
    gain = resum([r[base:] for r in (own, u1, u2, u3)])
    gain_ref[...] = (gain[0:4] + gain[4:8]) * SCALE


def sum_kernel(own_ref, r1_ref, r2_ref, r3_ref, out_ref):
    total = own_ref[...]
    for ref in (r1_ref, r2_ref, r3_ref):
        total = total + ref[...].astype(F32)
    out_ref[...] = (total * SCALE).T


def shift(x, axis, size, k, wrap=True):
    pairs = [(i, (i + k) % size) for i in range(size) if wrap or 0 <= i + k < size]
    return lax.ppermute(x, axis, pairs)


def swap_cores(x):
    return lax.ppermute(x, "core", [(0, 1), (1, 0)])


def body(queries, keys, values, gain, out_weight, out_cotangent):
    own = out_cotangent
    fwd, bwd = shift(own, "tp", RING, 1), shift(own, "tp", RING, -1)
    slices = ((32, 16, HEAD_DIM), BF)
    state, state_token = call(state_kernel, [slices, TOKEN], 2, 1 << 27)(keys, values)
    states = lax.all_to_all(state, BLOCKS, 0, 0, tiled=True)
    others = [shift(out_weight, "y", 4, k) for k in (1, 2, 3)]
    column, column_token = call(
        pack_kernel,
        [((4, 128, WIDTH), BF), TOKEN],
        0,
        1 << 20,
        6,
        [pltpu.VMEM(*TOKEN), pltpu.SemaphoreType.DMA((5,))],
        True,
    )(fwd, bwd, out_weight, *others)
    fwd, bwd = tie((fwd, bwd), (state_token, column_token))
    chunks = [own, fwd, bwd]

    fwd, bwd = shift(fwd, "tp", RING, 1), shift(bwd, "tp", RING, -1)
    priors, scan_token = call(scan_kernel, [slices, TOKEN], 1, 1 << 20)(states)
    prior = lax.all_to_all(priors, BLOCKS, 0, 0, tiled=True).reshape(STATE)
    column_low, column_high = shift(column, "dp", 4, 1), shift(column, "dp", 4, -1)
    gain_row = gain.reshape(1, WIDTH)
    att, gated = call(norm_kernel, [(SQUARE, F32), (SQUARE, BF)], 5, 1 << 30)(
        queries, keys, values, gain_row, prior
    )
    relay = ((2, 128, WIDTH), BF)
    relay_low, relay_high = call(
        relay_rows_kernel, [relay, relay], 0, 0, 4, [pltpu.SemaphoreType.DMA((2,))], True
    )(fwd, bwd, column_low, column_high)
    fwd, bwd = tie((fwd, bwd), (scan_token,))
    chunks += [fwd, bwd]

    fwd, bwd = shift(fwd, "tp", RING, 1), shift(bwd, "tp", RING, -1)
    relay_low, relay_high = shift(relay_low, "dp", 4, 1), shift(relay_high, "dp", 4, -1)
    half = ((TOKENS // 2, WIDTH), BF)
    last_low, last_high, weight = call(
        turn_kernel, [half, half, ((4, 4, 128, WIDTH), BF)], 7, 1 << 20, 1
    )(gated, fwd, bwd, column, column_low, column_high, relay_low, relay_high)
    chunks += [fwd, bwd]
    last_low, last_high = shift(last_low, "tp", RING, 1), shift(last_high, "tp", RING, -1)
    weight_other = swap_cores(weight)

    wide = ((8, WIDTH, WIDTH), BF)
    partial_sum, parts, weight_last = call(
        early_kernel,
        [(SQUARE, F32), wide, ((2, WIDTH, WIDTH), BF)],
        3,
        1 << 33,
        7,
        [pltpu.VMEM((7, TOKENS, WIDTH), BF), pltpu.SemaphoreType.DMA((7,))],
    )(*chunks, gated, weight, weight_other)
    last, other = call(last_kernel, [(SQUARE, BF), ((4, WIDTH, WIDTH), BF)], 4, 1 << 29)(
        last_low, last_high, gated, parts
    )
    ga, send, grad_token = call(
        grad_kernel,
        [(SQUARE, BF), (STATE_GAIN, BF), TOKEN],
        7,
        1 << 30,
        0,
        [pltpu.VMEM(SQUARE, F32)],
    )(last_low, last_high, weight_last, partial_sum, queries, att, gain_row)
    quarter, eighth = ((4, WIDTH, 128), BF), ((2 * WIDTH, 128), BF)
    part, up, down, low, high = call(
        combine_kernel,
        [quarter, quarter, quarter, eighth, eighth],
        4,
        1 << 20,
        0,
        [pltpu.VMEM(SQUARE, BF)],
    )(grad_token, parts, swap_cores(other), last)
    total, after = call(row_back_kernel, [(STATE_GAIN, BF), (STATE, F32)], 4, 1 << 22)(
        send, *[shift(send, "dp", 4, -k) for k in (1, 2, 3)]
    )
    other = swap_cores(total)
    (both,) = call(pair_back_kernel, [(STATE_GAIN, BF)], 2, 1 << 22)(total, other)
    up, down = call(relay_kernel, [quarter, quarter], 4, 1 << 20, 1)(
        both, up, down, shift(low, "dp", 4, 1), shift(high, "dp", 4, -1)
    )
    query_grad, key_part, value_part, token = call(
        post_kernel, [(SQUARE, BF), (SQUARE, F32), (SQUARE, F32), TOKEN], 5, 1 << 31
    )(queries, keys, values, ga, prior)
    block = (WIDTH, 128)
    part, up, away, down = call(
        column_kernel,
        [(block, F32), (block, BF), (block, BF), (block, BF)],
        4,
        1 << 20,
        0,
        [pltpu.VMEM((4, WIDTH, 128), F32)],
    )(token, part, shift(up, "dp", 4, 1), shift(down, "dp", 4, -1))
    (weight_grad,) = call(sum_kernel, [((128, WIDTH), F32)], 4, 1 << 20)(
        part, shift(up, "y", 4, 1), shift(away, "y", 4, 2), shift(down, "y", 4, -1)
    )
    upper = [shift(both, "y", 4, -k) for k in (1, 2, 3)]
    key_grad, value_grad, gain_sum = call(
        final_kernel, [(SQUARE, BF), (SQUARE, BF), ((HEADS, HEAD_DIM), F32)], 10, 1 << 28, 1
    )(down, keys, values, key_part, value_part, after, other, both, *upper)
    gain_grad = gain_sum.reshape(WIDTH)
    return query_grad, key_grad, value_grad, gain_grad, weight_grad


def solution(mesh):
    grid = Mesh(mesh.devices.reshape(4, 2, RING, 4), ("y", "core", "tp", "dp"))
    rows = P(("y", "core", "dp"), "tp")
    return jax.shard_map(
        body,
        mesh=grid,
        in_specs=(rows, rows, rows, P("tp"), rows, rows),
        out_specs=(rows, rows, rows, P("tp"), rows),
        check_vma=False,
    )
```

```python
import math

import jax
import jax.numpy as jnp
from jax import lax
from jax.experimental import pallas as pl
from jax.experimental.pallas import tpu as pltpu
from jax.sharding import Mesh
from jax.sharding import PartitionSpec as P

HEAD_DIM = 128
HEADS = 4
TOKENS = 512
WIDTH = 512
RING = 8
EPS = 1e-06
SCALE = 1.0 / math.sqrt(16384.0)
BF = jnp.bfloat16
F32 = jnp.float32
PLANE = ("y", "dp")
BLOCKS = ("y", "core", "dp")
VMEM_LIMIT = 24 * 1024 * 1024
STATE = (HEADS * HEAD_DIM, HEAD_DIM)
STATE_GAIN = (HEADS * HEAD_DIM + 16, HEAD_DIM)
SQUARE = (TOKENS, WIDTH)
TOKEN = ((8, HEAD_DIM), jnp.float32)

NN = ((1,), (0,))
NT = ((1,), (1,))
TN = ((0,), (0,))


def dot(a, b, dims):
    return lax.dot_general(a, b, (dims, ((), ())), preferred_element_type=F32)


def span(h):
    return pl.ds(pl.multiple_of(h * HEAD_DIM, HEAD_DIM), HEAD_DIM)


def each(count, step, unroll=1):
    lax.fori_loop(0, count, lambda i, carry: (step(i), carry)[1], 0, unroll=unroll)


def causal_mask():
    rows = lax.broadcasted_iota(jnp.int32, (TOKENS, TOKENS), 0)
    cols = lax.broadcasted_iota(jnp.int32, (TOKENS, TOKENS), 1)
    return rows >= cols


def call(kernel, out, n_in, flops, any_in=0, scratch=(), any_out=False):
    limit = VMEM_LIMIT if flops > 1 << 22 else VMEM_LIMIT // 2
    vmem = pl.BlockSpec(memory_space=pltpu.VMEM)
    anys = pl.BlockSpec(memory_space=pl.ANY)
    return pl.pallas_call(
        kernel,
        out_shape=tuple(jax.ShapeDtypeStruct(s, d) for s, d in out),
        in_specs=[anys] * any_in + [vmem] * n_in,
        out_specs=tuple(anys if any_out else vmem for _ in out),
        scratch_shapes=scratch,
        compiler_params=pltpu.CompilerParams(vmem_limit_bytes=limit),
        cost_estimate=pl.CostEstimate(flops=flops, bytes_accessed=4 << 20, transcendentals=0),
    )


def state_kernel(k_ref, v_ref, out_ref, token_ref):
    token_ref[...] = jnp.zeros(TOKEN[0], F32)

    def step(h):
        state = dot(k_ref[:, span(h)], v_ref[:, span(h)], TN).astype(BF)
        out_ref[pl.ds(h * 8, 8)] = state.reshape(8, 16, HEAD_DIM)

    each(HEADS, step)


def scan_kernel(in_ref, out_ref, token_ref):
    token_ref[...] = jnp.zeros(TOKEN[0], F32)
    total = jnp.zeros((16, HEAD_DIM), F32)
    for c in range(32):
        out_ref[c] = total.astype(BF)
        total = total + in_ref[c].astype(F32)


def when(flag):
    return jnp.where(flag, 1.0, 0.0).astype(F32)


def norm_kernel(q_ref, k_ref, v_ref, gain_ref, prior_ref, att_ref, gated_ref):
    mask = causal_mask()

    def step(h):
        cols = span(h)
        scores = dot(q_ref[:, cols], k_ref[:, cols], NT)
        scores = jnp.where(mask, scores, 0.0).astype(BF)
        att = dot(scores, v_ref[:, cols], NN) + dot(q_ref[:, cols], prior_ref[cols], NN)
        att_ref[:, cols] = att
        inverse = lax.rsqrt(jnp.mean(att * att, axis=-1, keepdims=True) + EPS)
        gated = (att * inverse * gain_ref[:, cols]).astype(BF)
        gated_ref[cols, :] = gated.T

    each(HEADS, step, 4)


def is_same():
    return lax.rem(lax.axis_index("tp"), 2) == lax.axis_index("core")


def row_of(k):
    return lax.div(lax.rem(lax.axis_index("tp") + k + RING, RING), 2)


EVENS = (0, 2, -2, 4)
ODDS = (1, -1, 3, -3)


ORDER = (0, 2, -2, 1, -1, 3, -3)


def early_kernel(*refs):
    own, f1, b1, f2, b2, f3, b3, gated_ref, wm_ref, wo_ref = refs[:10]
    sum_ref, part_ref, weight_ref, rows, sems = refs[10:]
    copies = []
    for n, ref in enumerate((own, b2, f2, b1, f1, b3, f3)):
        copies.append(pltpu.make_async_copy(ref, rows.at[n], sems.at[n]))
    for c in copies:
        c.start()
    for c in copies:
        c.wait()
    sum_ref[...] = jnp.zeros(SQUARE, F32)
    same = is_same()

    def offset(n):
        k = jnp.int32(ORDER[-1])
        for i in range(len(ORDER) - 1):
            k = jnp.where(n == i, ORDER[i], k)
        return k

    def fetch(even, k, slot):
        mine = jnp.logical_not(jnp.logical_xor(same, even))
        y = row_of(k)

        @pl.when(mine)
        def _():
            weight_ref[slot] = wm_ref[y].reshape(SQUARE)

        @pl.when(jnp.logical_not(mine))
        def _():
            weight_ref[slot] = wo_ref[y].reshape(SQUARE)

    def part(n):
        part_ref[jnp.where(n < 3, n, n + 1)] = dot(gated_ref[...], rows[n], NN).astype(BF)

    def step(i):
        n = 2 * i
        for m in range(2):
            fetch(n + m < 3, offset(n + m), m)
            part(n + m)
        first = dot(rows[n], weight_ref[0], NN)
        sum_ref[...] += first + dot(rows[n + 1], weight_ref[1], NN)

    each(3, step)
    fetch(jnp.bool_(False), jnp.int32(ORDER[6]), 0)
    part(jnp.int32(6))
    sum_ref[...] += dot(rows[6], weight_ref[0], NN)
    fetch(jnp.bool_(True), jnp.int32(4), 0)


def last_kernel(low_ref, high_ref, gated_ref, part_ref, last_ref, other_ref):
    half = TOKENS // 2
    last = dot(gated_ref[:, 0:half], low_ref[...], NN)
    last_ref[...] = (last + dot(gated_ref[:, half:TOKENS], high_ref[...], NN)).astype(BF)
    base = jnp.where(is_same(), 4, 0)

    def step(s):
        other_ref[s] = part_ref[base + s]

    each(3, step)

    @pl.when(is_same())
    def _():
        other_ref[3] = part_ref[7]

    @pl.when(jnp.logical_not(is_same()))
    def _():
        other_ref[3] = last_ref[...]


def grad_kernel(
    low_ref, high_ref, weight_ref, sum_ref, q_ref, att_ref, gain_ref, ga_ref, send_ref, token_ref, acc
):
    token_ref[...] = jnp.zeros(TOKEN[0], F32)
    half = TOKENS // 2
    acc[0:half] = sum_ref[0:half] + dot(low_ref[...], weight_ref[0], NN)
    acc[half:TOKENS] = sum_ref[half:TOKENS] + dot(high_ref[...], weight_ref[0], NN)
    grad_rows(acc, q_ref, att_ref, gain_ref, ga_ref, send_ref)


def combine_kernel(
    after_ref, part_ref, got_ref, last_ref, own_ref, up_ref, down_ref, low_ref, high_ref, rows
):
    place = lax.axis_index("dp")
    same = is_same()
    base = jnp.where(same, 0, 4)

    def step(s):
        late = jnp.logical_and(same, s == 3)

        @pl.when(late)
        def _():
            rows[...] = (last_ref[...].astype(F32) + got_ref[s].astype(F32)).astype(BF)

        @pl.when(jnp.logical_not(late))
        def _():
            rows[...] = (part_ref[base + s].astype(F32) + got_ref[s].astype(F32)).astype(BF)

        blocks = []
        for d in range(4):
            start = pl.multiple_of(lax.rem(place + d, 4) * 128, 128)
            blocks.append(rows[:, pl.ds(start, 128)])
        own_ref[s], up_ref[s], down_ref[s] = blocks[0], blocks[1], blocks[3]
        at = pl.ds(pl.multiple_of(s * 256, 256), 256)
        low_ref[at], high_ref[at] = blocks[2][0:256], blocks[2][256:512]

    each(4, step)


def pack_kernel(
    after1_ref, after2_ref, own_ref, r1_ref, r2_ref, r3_ref, out_ref, token_out, token, sems
):
    token[...] = jnp.zeros(TOKEN[0], F32)
    y = lax.axis_index("y")
    copies = [pltpu.make_async_copy(token, token_out, sems.at[4])]
    for k, ref in enumerate((own_ref, r1_ref, r2_ref, r3_ref)):
        copies.append(pltpu.make_async_copy(ref, out_ref.at[lax.rem(y + 4 - k, 4)], sems.at[k]))
    for c in copies:
        c.start()
    for c in copies:
        c.wait()


def relay_rows_kernel(after1_ref, after2_ref, low_ref, high_ref, low_out, high_out, sems):
    low = pltpu.make_async_copy(low_ref.at[0:2], low_out, sems.at[0])
    high = pltpu.make_async_copy(high_ref.at[2:4], high_out, sems.at[1])
    low.start()
    high.start()
    low.wait()
    high.wait()


def turn_kernel(
    after_ref, fwd_ref, bwd_ref, own_ref, low_ref, high_ref, far_low_ref, far_high_ref,
    fwd_out, bwd_out, out_ref,
):
    fwd_out[...] = fwd_ref[0 : TOKENS // 2]
    bwd_out[...] = bwd_ref[TOKENS // 2 : TOKENS]
    x = lax.axis_index("dp")
    for k, ref in ((0, own_ref), (3, low_ref), (1, high_ref)):
        for y in range(4):
            out_ref[y, lax.rem(x + k, 4)] = ref[y]
    for y in range(2):
        out_ref[y, lax.rem(x + 2, 4)] = far_low_ref[y]
        out_ref[2 + y, lax.rem(x + 2, 4)] = far_high_ref[y]


def tie(values, deps):
    def kernel(*refs):
        pass

    n = len(values)
    anys = pl.BlockSpec(memory_space=pl.ANY)
    return pl.pallas_call(
        kernel,
        out_shape=tuple(jax.ShapeDtypeStruct(v.shape, v.dtype) for v in values),
        in_specs=[anys] * (n + len(deps)),
        out_specs=(anys,) * n,
        input_output_aliases={i: i for i in range(n)},
        compiler_params=pltpu.CompilerParams(vmem_limit_bytes=1 << 20),
        cost_estimate=pl.CostEstimate(flops=0, bytes_accessed=0, transcendentals=0),
    )(*values, *deps)


def relay_kernel(after_ref, up_ref, down_ref, low_ref, high_ref, up_out, down_out):
    def step(y):
        rows = pl.ds(pl.multiple_of(y * 256, 256), 256)
        up_out[y, 0:256] = (up_ref[y, 0:256].astype(F32) + low_ref[rows].astype(F32)).astype(BF)
        up_out[y, 256:512] = up_ref[y, 256:512]
        down_out[y, 0:256] = down_ref[y, 0:256]
        low = down_ref[y, 256:512].astype(F32) + high_ref[rows].astype(F32)
        down_out[y, 256:512] = low.astype(BF)

    each(4, step)


def column_kernel(after_ref, own_ref, a_ref, b_ref, own_out, up_out, far_out, down_out, rows):
    same = is_same()

    def step(s):
        k = jnp.where(s == 3, 4, jnp.where(s == 2, -2, s * 2))
        odd = jnp.where(s == 3, -3, jnp.where(s == 2, 3, 1 - 2 * s))
        y = row_of(jnp.where(same, k, odd))
        total = own_ref[s].astype(F32) + a_ref[s].astype(F32) + b_ref[s].astype(F32)
        rows[lax.rem(y + 4 - lax.axis_index("y"), 4)] = total

    each(4, step)
    own_out[...] = rows[0]
    up_out[...] = rows[1].astype(BF)
    far_out[...] = rows[2].astype(BF)
    down_out[...] = rows[3].astype(BF)


def grad_rows(own_ref, q_ref, att_ref, gain_ref, ga_ref, send_ref):
    base = HEADS * HEAD_DIM
    rows = lax.broadcasted_iota(jnp.int32, (16, HEAD_DIM), 0)

    def step(h, sums):
        att = att_ref[:, span(h)]
        inverse = lax.rsqrt(jnp.mean(att * att, axis=-1, keepdims=True) + EPS)
        normed = att * inverse
        grad = own_ref[:, span(h)]
        part = jnp.sum(grad * normed, axis=0, keepdims=True)
        high = part.astype(BF).astype(F32)
        sums = sums + jnp.where(rows == h, high, 0.0) + jnp.where(rows == 4 + h, part - high, 0.0)
        grad = grad * gain_ref[:, span(h)]
        grad = (grad - normed * jnp.mean(grad * normed, axis=-1, keepdims=True)) * inverse
        grad = grad.astype(BF)
        ga_ref[:, span(h)] = grad
        send_ref[span(h)] = dot(q_ref[:, span(h)], grad, TN).astype(BF)
        return sums

    sums = lax.fori_loop(0, HEADS, step, jnp.zeros((16, HEAD_DIM), F32), unroll=4)
    send_ref[base:] = sums.astype(BF)


def resum(parts):
    total = sum(p.astype(F32) for p in parts)
    gain = total[0:4] + total[4:8]
    high = gain.astype(BF).astype(F32)
    return jnp.concatenate([high, gain - high, jnp.zeros((8, HEAD_DIM), F32)], axis=0)


def row_back_kernel(own_ref, r1_ref, r2_ref, r3_ref, total_ref, after_ref):
    x = lax.axis_index("dp")
    base = HEADS * HEAD_DIM
    r1, r2, r3 = (r[0:base].astype(F32) for r in (r1_ref, r2_ref, r3_ref))
    after_ref[...] = r1 * when(x <= 2) + r2 * when(x <= 1) + r3 * when(x <= 0)
    total_ref[0:base] = (own_ref[0:base].astype(F32) + r1 + r2 + r3).astype(BF)
    total_ref[base:] = resum([r[base:] for r in (own_ref, r1_ref, r2_ref, r3_ref)]).astype(BF)


def pair_back_kernel(total_ref, other_ref, out_ref):
    base = HEADS * HEAD_DIM
    out_ref[0:base] = (total_ref[0:base].astype(F32) + other_ref[0:base].astype(F32)).astype(BF)
    out_ref[base:] = resum([total_ref[base:], other_ref[base:]]).astype(BF)


def post_kernel(q_ref, k_ref, v_ref, ga_ref, prior_ref, qg_ref, kp_ref, vp_ref, token_ref):
    token_ref[...] = jnp.zeros(TOKEN[0], F32)
    mask = causal_mask()

    def step(h):
        cols = span(h)
        q, k, v, ga = q_ref[:, cols], k_ref[:, cols], v_ref[:, cols], ga_ref[:, cols]
        scores = jnp.where(mask, dot(q, k, NT), 0.0).astype(BF)
        vp_ref[:, cols] = dot(scores, ga, TN)
        back = jnp.where(mask, dot(ga, v, NT), 0.0).astype(BF)
        qg_ref[:, cols] = (dot(back, k, NN) + dot(ga, prior_ref[cols], NT)).astype(BF)
        kp_ref[:, cols] = dot(back, q, TN)

    each(HEADS, step)


def final_kernel(
    after_last_ref, k_ref, v_ref, kp_ref, vp_ref, after_ref, other_ref, own, u1, u2, u3, kg_ref, vg_ref, gain_ref
):
    base = HEADS * HEAD_DIM
    y = lax.axis_index("y")
    first = when(lax.axis_index("core") == 0)

    def step(h):
        cols = span(h)
        later = after_ref[cols] + other_ref[cols].astype(F32) * first
        later = later + u1[cols].astype(F32) * when(y <= 2) + u2[cols].astype(F32) * when(y <= 1)
        later = (later + u3[cols].astype(F32) * when(y <= 0)).astype(BF)
        kg_ref[:, cols] = (kp_ref[:, cols] + dot(v_ref[:, cols], later, NT)).astype(BF)
        vg_ref[:, cols] = (vp_ref[:, cols] + dot(k_ref[:, cols], later, NN)).astype(BF)

    each(HEADS, step, 2)
    gain = resum([r[base:] for r in (own, u1, u2, u3)])
    gain_ref[...] = (gain[0:4] + gain[4:8]) * SCALE


def sum_kernel(own_ref, r1_ref, r2_ref, r3_ref, out_ref):
    total = own_ref[...]
    for ref in (r1_ref, r2_ref, r3_ref):
        total = total + ref[...].astype(F32)
    out_ref[...] = (total * SCALE).T


def shift(x, axis, size, k, wrap=True):
    pairs = [(i, (i + k) % size) for i in range(size) if wrap or 0 <= i + k < size]
    return lax.ppermute(x, axis, pairs)


def swap_cores(x):
    return lax.ppermute(x, "core", [(0, 1), (1, 0)])


def body(queries, keys, values, gain, out_weight, out_cotangent):
    own = out_cotangent
    fwd, bwd = shift(own, "tp", RING, 1), shift(own, "tp", RING, -1)
    slices = ((32, 16, HEAD_DIM), BF)
    state, state_token = call(state_kernel, [slices, TOKEN], 2, 1 << 27)(keys, values)
    states = lax.all_to_all(state, BLOCKS, 0, 0, tiled=True)
    others = [shift(out_weight, "y", 4, k) for k in (1, 2, 3)]
    column, column_token = call(
        pack_kernel,
        [((4, 128, WIDTH), BF), TOKEN],
        0,
        1 << 20,
        6,
        [pltpu.VMEM(*TOKEN), pltpu.SemaphoreType.DMA((5,))],
        True,
    )(fwd, bwd, out_weight, *others)
    fwd, bwd = tie((fwd, bwd), (state_token, column_token))
    chunks = [own, fwd, bwd]

    fwd, bwd = shift(fwd, "tp", RING, 1), shift(bwd, "tp", RING, -1)
    priors, scan_token = call(scan_kernel, [slices, TOKEN], 1, 1 << 20)(states)
    prior = lax.all_to_all(priors, BLOCKS, 0, 0, tiled=True).reshape(STATE)
    column_low, column_high = shift(column, "dp", 4, 1), shift(column, "dp", 4, -1)
    gain_row = gain.reshape(1, WIDTH)
    att, gated = call(norm_kernel, [(SQUARE, F32), (SQUARE, BF)], 5, 1 << 30)(
        queries, keys, values, gain_row, prior
    )
    relay = ((2, 128, WIDTH), BF)
    relay_low, relay_high = call(
        relay_rows_kernel, [relay, relay], 0, 0, 4, [pltpu.SemaphoreType.DMA((2,))], True
    )(fwd, bwd, column_low, column_high)
    fwd, bwd = tie((fwd, bwd), (scan_token,))
    chunks += [fwd, bwd]

    fwd, bwd = shift(fwd, "tp", RING, 1), shift(bwd, "tp", RING, -1)
    relay_low, relay_high = shift(relay_low, "dp", 4, 1), shift(relay_high, "dp", 4, -1)
    half = ((TOKENS // 2, WIDTH), BF)
    last_low, last_high, weight = call(
        turn_kernel, [half, half, ((4, 4, 128, WIDTH), BF)], 7, 1 << 20, 1
    )(gated, fwd, bwd, column, column_low, column_high, relay_low, relay_high)
    chunks += [fwd, bwd]
    last_low, last_high = shift(last_low, "tp", RING, 1), shift(last_high, "tp", RING, -1)
    weight_other = swap_cores(weight)

    wide = ((8, WIDTH, WIDTH), BF)
    partial_sum, parts, weight_last = call(
        early_kernel,
        [(SQUARE, F32), wide, ((2, WIDTH, WIDTH), BF)],
        3,
        1 << 33,
        7,
        [pltpu.VMEM((7, TOKENS, WIDTH), BF), pltpu.SemaphoreType.DMA((7,))],
    )(*chunks, gated, weight, weight_other)
    last, other = call(last_kernel, [(SQUARE, BF), ((4, WIDTH, WIDTH), BF)], 4, 1 << 29)(
        last_low, last_high, gated, parts
    )
    ga, send, grad_token = call(
        grad_kernel,
        [(SQUARE, BF), (STATE_GAIN, BF), TOKEN],
        7,
        1 << 30,
        0,
        [pltpu.VMEM(SQUARE, F32)],
    )(last_low, last_high, weight_last, partial_sum, queries, att, gain_row)
    quarter, eighth = ((4, WIDTH, 128), BF), ((2 * WIDTH, 128), BF)
    part, up, down, low, high = call(
        combine_kernel,
        [quarter, quarter, quarter, eighth, eighth],
        4,
        1 << 20,
        0,
        [pltpu.VMEM(SQUARE, BF)],
    )(grad_token, parts, swap_cores(other), last)
    total, after = call(row_back_kernel, [(STATE_GAIN, BF), (STATE, F32)], 4, 1 << 22)(
        send, *[shift(send, "dp", 4, -k) for k in (1, 2, 3)]
    )
    other = swap_cores(total)
    (both,) = call(pair_back_kernel, [(STATE_GAIN, BF)], 2, 1 << 22)(total, other)
    up, down = call(relay_kernel, [quarter, quarter], 4, 1 << 20, 1)(
        both, up, down, shift(low, "dp", 4, 1), shift(high, "dp", 4, -1)
    )
    query_grad, key_part, value_part, token = call(
        post_kernel, [(SQUARE, BF), (SQUARE, F32), (SQUARE, F32), TOKEN], 5, 1 << 31
    )(queries, keys, values, ga, prior)
    block = (WIDTH, 128)
    part, up, away, down = call(
        column_kernel,
        [(block, F32), (block, BF), (block, BF), (block, BF)],
        4,
        1 << 20,
        0,
        [pltpu.VMEM((4, WIDTH, 128), F32)],
    )(token, part, shift(up, "dp", 4, 1), shift(down, "dp", 4, -1))
    (weight_grad,) = call(sum_kernel, [((128, WIDTH), F32)], 4, 1 << 20)(
        part, shift(up, "y", 4, 1), shift(away, "y", 4, 2), shift(down, "y", 4, -1)
    )
    upper = [shift(both, "y", 4, -k) for k in (1, 2, 3)]
    key_grad, value_grad, gain_sum = call(
        final_kernel, [(SQUARE, BF), (SQUARE, BF), ((HEADS, HEAD_DIM), F32)], 10, 1 << 28, 1
    )(down, keys, values, key_part, value_part, after, other, both, *upper)
    gain_grad = gain_sum.reshape(WIDTH)
    return query_grad, key_grad, value_grad, gain_grad, weight_grad


def solution(mesh):
    grid = Mesh(mesh.devices.reshape(4, 2, RING, 4), ("y", "core", "tp", "dp"))
    rows = P(("y", "core", "dp"), "tp")
    return jax.shard_map(
        body,
        mesh=grid,
        in_specs=(rows, rows, rows, P("tp"), rows, rows),
        out_specs=(rows, rows, rows, P("tp"), rows),
        check_vma=False,
    )
```
